256 devices in a mesh: row: 16 (over y, z_hi, core), col: 16 (over z_lo, x).
Axes of the slice: x: 4, y: 4, z: 8 (z_hi: 2, z_lo: 4; z = z_hi * 4 + z_lo), core: 2. Of those that a mesh axis runs over, the one named last changes fastest.
Arguments:
- grad: bfloat16 [5120, 8192], P('row', 'col'), may hold values from -6 to 6
- left_basis: bfloat16 [5120, 5120], P('row', 'col'), may hold values from -0.078125 to 0.078125
- right_basis: bfloat16 [8192, 8192], P('row', 'col'), may hold values from -0.0625 to 0.0625
- first_moment: float32 [5120, 8192], P('row', 'col'), may hold values from -3 to 3
- second_moment: float32 [5120, 8192], P('row', 'col'), may hold values from 0.05 to 2
Outputs:
- update: float32 [5120, 8192], P('row', 'col')
- first_new: float32 [5120, 8192], P('row', 'col')
- second_new: float32 [5120, 8192], P('row', 'col')
The draws below stay inside these ranges and needn't reach their ends.
All inputs are finite; a program needn't handle non-finite values.
Results may differ from the reference program's by a relative error of at most 0.0041.
Values may be sent and summed in bfloat16 or wider, within the bound.
No kernel may reach another device: no remote copies, remote signals or barrier semaphores. Data moves between devices by JAX's collectives and lax.ppermute only.
A program may use at most 128 MiB of HBM per device.

```python
import math
import jax
import jax.numpy as jnp

D = 5120
BLOCK = 8192


def raised(values, stream_key, source, target, blocks, factor):
    owner, partner = [(jnp.arange(values.shape[axis_at]) // (values.shape[axis_at] // blocks)).reshape([-1 if axis == axis_at else 1 for axis in range(values.ndim)]) for axis_at in (source, target)]
    chosen = jax.random.permutation(stream_key, blocks)[partner]
    strong = (owner == chosen) | (owner == (partner + blocks // 2) % blocks)
    return jnp.where(strong, factor * values, values)


def block_scale(stream_key, dims, split, smallest, high):
    def one(dim, shards_of):
        draws = jax.random.uniform(jax.random.fold_in(jax.random.fold_in(stream_key, 6), dim), (shards_of,), jnp.float32, smallest / len(split), high / len(split))
        return jnp.repeat(jnp.exp(draws), dims[dim] // shards_of).reshape((-1,) + (1,) * (len(dims) - dim - 1))

    loudness = one(*split[0])
    for cut in split[1:]:
        loudness = loudness * one(*cut)
    return loudness


def noise(key, dims, width, reach, split=(), dtype=jnp.bfloat16):
    gain = block_scale(key, dims, split, -0.22, 0.18) if split else 1.0
    values = jax.random.normal(key, dims, jnp.float32) * width * gain
    return jnp.minimum(jnp.maximum(values, -reach), reach).astype(dtype)


def heavy_noise(stream_key, shape, width, reach, cuts, heavy, dtype=jnp.bfloat16):
    values = width * jax.random.normal(stream_key, shape, jnp.float32)
    if cuts:
        values = values * block_scale(stream_key, shape, cuts, -0.22, 0.18)
    return jnp.clip(raised(values, jax.random.fold_in(stream_key, 3), *heavy), -reach, reach).astype(dtype)


def setup_inputs(seed: int = 0) -> dict:
    splits = jax.random.split(jax.random.key(seed), 6)
    grad = heavy_noise(splits[0], (D, BLOCK), 1.0, 6.0, ((0, 16), (1, 16)), (0, 1, 16, 2.0))
    left_basis = noise(splits[1], (D, D), D ** -0.5, 0.078125, ((0, 16), (1, 16)))
    right_basis = noise(splits[2], (BLOCK, BLOCK), BLOCK ** -0.5, 0.0625, ((0, 16), (1, 16)))
    first_moment = noise(splits[3], (D, BLOCK), 0.5, 3.0, ((0, 16), (1, 16)), jnp.float32)
    second_moment = jnp.clip(jnp.exp(math.log(2.0) - 3.6888794 * jax.random.uniform(splits[4], (D, BLOCK), jnp.float32) ** block_scale(splits[4], (D, BLOCK), ((0, 16), (1, 16)), -0.2, 0.2)), 0.05, 2.0)
    return {"grad": grad, "left_basis": left_basis, "right_basis": right_basis, "first_moment": first_moment, "second_moment": second_moment}


beta_one = 0.9
beta_two = 0.95
corr_one = 1.0 - 0.9 ** 10
corr_two = 1.0 - 0.95 ** 10
eps_value = 1e-08

def reference(grad, left_basis, right_basis, first_moment, second_moment):
    rotated_in = jnp.dot(left_basis.T, grad, preferred_element_type=jnp.float32).astype(jnp.bfloat16)
    rotated = jnp.dot(rotated_in, right_basis, preferred_element_type=jnp.float32)
    first_new = beta_one * first_moment + (1.0 - beta_one) * rotated
    second_new = beta_two * second_moment + (1.0 - beta_two) * rotated * rotated
    normed = (first_new / corr_one / (jnp.sqrt(second_new / corr_two) + eps_value)).astype(jnp.bfloat16)
    back = jnp.dot(normed, right_basis.T, preferred_element_type=jnp.float32).astype(jnp.bfloat16)
    update = jnp.dot(left_basis, back, preferred_element_type=jnp.float32)
    return (update, first_new, second_new)
```

```python
import jax
import jax.numpy as jnp
from jax import lax
from jax.sharding import Mesh
from jax.sharding import PartitionSpec as P

beta_one = 0.9
beta_two = 0.95
corr_one = 1.0 - 0.9**10
corr_two = 1.0 - 0.95**10
eps_value = 1e-08

RING = ("zh", "zl")


def shift(arr, axes, size, by):
    return lax.ppermute(arr, axes, [(i, (i + by) % size) for i in range(size)])


def pick(arr, index):
    return lax.dynamic_index_in_dim(arr, index, 0, keepdims=False)


def mm(left, right, left_dim, right_dim):
    return lax.dot_general(
        left, right, (((left_dim,), (right_dim,)), ((), ())), preferred_element_type=jnp.float32
    )


def ring_blocks(block):
    half = block.shape[0] // 2
    out = [(0, block)]
    up, down = block, block
    for s in range(1, 4):
        up = shift(up, RING, 8, 1)
        down = shift(down, RING, 8, -1)
        out += [(s, up), (-s, down)]
    far = jnp.concatenate([shift(up[:half], RING, 8, 1), shift(down[half:], RING, 8, -1)], axis=0)
    return out + [(4, far)]


def adam_moments(rotated, first_moment, second_moment):
    first_new = beta_one * first_moment + (1.0 - beta_one) * rotated
    second_new = beta_two * second_moment + (1.0 - beta_two) * rotated * rotated
    normed = (first_new / corr_one / (jnp.sqrt(second_new / corr_two) + eps_value)).astype(
        jnp.bfloat16
    )
    return (first_new, second_new, normed)


def body(grad, left_basis, right_basis, first_moment, second_moment):
    f32, bf16 = jnp.float32, jnp.bfloat16
    y, zh, core = lax.axis_index("y"), lax.axis_index("zh"), lax.axis_index("core")
    zl, x = lax.axis_index("zl"), lax.axis_index("x")
    z = zh * 4 + zl
    rows, cols = grad.shape
    lead, part = left_basis.shape[1], left_basis.shape[1] // 4

    quarters = left_basis.T.reshape(4, part, rows)
    own = [pick(quarters, zl)]
    for d in (1, 2, 3):
        own.append(shift(pick(quarters, (zl + d) % 4), "zl", 4, d))
    turned = jnp.zeros((4, part, rows), bf16)
    for d in range(4):
        turned = lax.dynamic_update_index_in_dim(turned, own[d], (zl - d) % 4, 0)
    turned = turned.reshape(4 * part, rows)
    panel = jnp.zeros((4, 4 * part, rows), bf16)
    for k in range(4):
        pairs = []
        for zs in range(2):
            for xs in range(4):
                pairs.append((zs * 4 + xs, (xs // 2) * 4 + ((zs * 2 + xs % 2) ^ k)))
        got = lax.ppermute(turned, ("zh", "x"), pairs)
        q = x ^ k
        panel = lax.dynamic_update_index_in_dim(panel, got, (q % 2) * 2 + q // 2, 0)
    panel = panel.reshape(2, 2, 4 * part, rows)

    gradient = jnp.zeros((4, 2, rows, cols), bf16)
    for s, block in ring_blocks(grad):
        gradient = lax.dynamic_update_slice(
            gradient, block[None, None], ((zl - s) % 4, ((z - s) % 8) // 4, 0, 0)
        )
    gradient = gradient.reshape(4, 2 * rows, cols)

    size = right_basis.shape[0]
    right = jnp.zeros((4, size, 4 * size), bf16)
    for s, block in ring_blocks(right_basis):
        zs = ((z - s) % 8) // 4
        other = shift(block, "core", 2, 1)
        for blk, cc in ((block, core), (other, 1 - core)):
            slot = (x - zs * 2 - cc) % 4
            right = lax.dynamic_update_slice(right, blk[None], (slot, 0, (s % 4) * size))
    right = right.reshape(4 * size, 4 * size)

    def rotate(which):
        pair = pick(panel, which)
        wide = jnp.concatenate([pair[0], pair[1]], axis=1)
        return jnp.stack([mm(wide, gradient[j], 1, 0) for j in range(4)])

    away = shift(rotate(1 - core), "core", 2, 1)
    summed = rotate(core) + away
    total = pick(summed, y)
    for d in (1, 2, 3):
        total = total + shift(pick(summed, (y + d) % 4).astype(bf16), "y", 4, d).astype(f32)
    rotated_in = total.astype(bf16)
    wide = jnp.concatenate(
        [rotated_in] + [shift(rotated_in, "x", 4, d) for d in (1, 2, 3)], axis=1
    )

    partial = mm(wide, right, 1, 0).reshape(4, part, 4 * cols)
    rotated = pick(partial, y)
    for d in (1, 2, 3):
        rotated = rotated + shift(pick(partial, (y + d) % 4).astype(bf16), "y", 4, d).astype(f32)
    rotated = rotated.astype(bf16)
    home = jnp.zeros((4, part, cols), bf16)
    for e in range(4):
        piece = rotated[:, e * cols : (e + 1) * cols]
        if e:
            piece = shift(piece, "zl", 4, -e)
        home = lax.dynamic_update_index_in_dim(home, piece, (zl + e) % 4, 0)
    first_new, second_new, normed = adam_moments(
        home.reshape(rows, cols).astype(f32), first_moment, second_moment
    )

    parts = normed.reshape(4, part, cols)
    got = [pick(parts, zl)]
    for e in (1, 2, 3):
        got.append(shift(pick(parts, (zl + e) % 4), "zl", 4, e))
    got = jnp.concatenate(got, axis=1)
    tall = jnp.zeros((4, part, 4 * cols), bf16)
    for d in range(4):
        piece = shift(got, "y", 4, d) if d else got
        tall = lax.dynamic_update_index_in_dim(tall, piece, (y - d) % 4, 0)
    back = mm(tall.reshape(4 * part, 4 * cols), right, 1, 1)
    total = back[:, :cols]
    for d in (1, 2, 3):
        total = total + shift(
            back[:, d * cols : (d + 1) * cols].astype(bf16), "x", 4, -d
        ).astype(f32)
    back = total.astype(bf16)

    full = jnp.zeros((4, 4 * part, cols), bf16)
    for d in range(4):
        piece = shift(back, "y", 4, d) if d else back
        full = lax.dynamic_update_index_in_dim(full, piece, (y - d) % 4, 0)
    mine = pick(panel, core)
    theirs = shift(pick(panel, 1 - core), "core", 2, 1)

    def unrotate(pair):
        flat = jnp.concatenate([pair[0], pair[1]], axis=1)
        return jnp.stack([mm(flat, full[j], 0, 0) for j in range(4)])

    away = shift(unrotate(theirs).astype(bf16), "core", 2, 1).astype(f32)
    summed = (unrotate(mine) + away).reshape(8, rows, cols)
    update = pick(summed, zl * 2 + zh)
    for t in (1, -1, 2, -2, 3, -3, 4):
        to = (z + t) % 8
        piece = pick(summed, (to % 4) * 2 + to // 4).astype(bf16)
        update = update + shift(piece, RING, 8, t).astype(f32)
    return (update, first_new, second_new)


def solution(mesh):
    names = ("y", "zh", "core", "zl", "x")
    fine = Mesh(mesh.devices.reshape(4, 2, 2, 4, 4), names)
    spec = P(("y", "zh", "core"), ("zl", "x"))
    return jax.shard_map(
        body, mesh=fine, in_specs=(spec,) * 5, out_specs=(spec,) * 3, check_vma=False
    )
```

```python
import jax
import jax.numpy as jnp
from jax import lax
from jax.experimental import pallas as pl
from jax.experimental.pallas import tpu as pltpu
from jax.sharding import Mesh
from jax.sharding import PartitionSpec as P

beta_one = 0.9
beta_two = 0.95
corr_one = 1.0 - 0.9**10
corr_two = 1.0 - 0.95**10
eps_value = 1e-08

RING = ("zh", "zl")


def shift(arr, axes, size, by):
    return lax.ppermute(arr, axes, [(i, (i + by) % size) for i in range(size)])


def pick(arr, index):
    return lax.dynamic_index_in_dim(arr, index, 0, keepdims=False)


def mm(left, right, left_dim, right_dim):
    return lax.dot_general(
        left, right, (((left_dim,), (right_dim,)), ((), ())), preferred_element_type=jnp.float32
    )


def tie(*values):
    return lax.optimization_barrier(values)


def turn_right(place, wide, right_own, right_far):
    rows, cols = wide[0].shape
    part = rows // 4

    def kernel(at, w0, w1, w2, w3, own, far, mine, far1, far2, far3, held, total):
        x, y, core = at[0], at[1], at[3]

        @pl.when(pl.program_id(0) == 0)
        def _():
            for d, ref in enumerate((w0, w1, w2, w3)):
                held[lax.rem(x + 4 - d, 4)] = ref[...]

        acc = jnp.zeros((rows, cols), jnp.float32)
        for which, ref in ((core, own), (1 - core, far)):
            for h in range(2):
                acc += jnp.dot(held[2 * h + which], ref[h, 0], preferred_element_type=jnp.float32)
        total[...] = acc.reshape(4, part, cols)
        mine[...] = total[y]
        for d, ref in ((1, far1), (2, far2), (3, far3)):
            ref[...] = total[lax.rem(y + d, 4)].astype(jnp.bfloat16)

    whole = pl.BlockSpec((rows, cols), lambda e, at: (0, 0))
    block = pl.BlockSpec((2, 1, cols, cols), lambda e, at: (0, lax.rem(at[2] + 4 - e, 4), 0, 0))
    out = pl.BlockSpec((part, cols), lambda e, at: (0, e))
    return pl.pallas_call(
        kernel,
        grid_spec=pltpu.PrefetchScalarGridSpec(
            num_scalar_prefetch=1,
            grid=(4,),
            in_specs=[whole] * 4 + [block] * 2,
            out_specs=[out] * 4,
            scratch_shapes=[
                pltpu.VMEM((4, rows, cols), jnp.bfloat16),
                pltpu.VMEM((4, part, cols), jnp.float32),
            ],
        ),
        out_shape=[jax.ShapeDtypeStruct((part, 4 * cols), jnp.float32)]
        + [jax.ShapeDtypeStruct((part, 4 * cols), jnp.bfloat16)] * 3,
        compiler_params=pltpu.CompilerParams(vmem_limit_bytes=40 * 2**20),
        cost_estimate=pl.CostEstimate(
            flops=32 * rows * cols * cols, bytes_accessed=32 * cols * cols, transcendentals=0
        ),
    )(place, *wide, right_own, right_far)


def turn_back(place, normed, right_own, right_far):
    part, long = normed[0].shape
    rows, cols = 4 * part, long // 4

    def kernel(at, n0, n1, n2, n3, own, far, mine, far1, far2, far3, held):
        x, y, zl, core = at[0], at[1], at[2], at[3]
        h = pl.program_id(0)

        @pl.when(h == 0)
        def _():
            for d, ref in enumerate((n0, n1, n2, n3)):
                held[lax.rem(y + 4 - d, 4)] = ref[...]

        for which, ref in ((core, own), (1 - core, far)):
            acc = jnp.zeros((rows, cols), jnp.float32)
            for e in range(4):
                acc += lax.dot_general(
                    held[:, :, e * cols : (e + 1) * cols].reshape(rows, cols),
                    ref[0, lax.rem(zl + 4 - e, 4)],
                    (((1,), (1,)), ((), ())),
                    preferred_element_type=jnp.float32,
                )
            slot = lax.rem(2 * h + which + 4 - x, 4)

            @pl.when(slot == 0)
            def _():
                mine[...] = acc

            for d, to in ((1, far1), (2, far2), (3, far3)):

                @pl.when(slot == d)
                def _():
                    to[...] = acc.astype(jnp.bfloat16)

    whole = pl.BlockSpec((part, long), lambda h, at: (0, 0))
    block = pl.BlockSpec((1, 4, cols, cols), lambda h, at: (h, 0, 0, 0))
    out = pl.BlockSpec((rows, cols), lambda h, at: (0, 0))
    return pl.pallas_call(
        kernel,
        grid_spec=pltpu.PrefetchScalarGridSpec(
            num_scalar_prefetch=1,
            grid=(2,),
            in_specs=[whole] * 4 + [block] * 2,
            out_specs=[out] * 4,
            scratch_shapes=[pltpu.VMEM((4, part, long), jnp.bfloat16)],
        ),
        out_shape=[jax.ShapeDtypeStruct((rows, cols), jnp.float32)]
        + [jax.ShapeDtypeStruct((rows, cols), jnp.bfloat16)] * 3,
        compiler_params=pltpu.CompilerParams(vmem_limit_bytes=40 * 2**20),
        cost_estimate=pl.CostEstimate(
            flops=32 * rows * cols * cols, bytes_accessed=32 * cols * cols, transcendentals=0
        ),
    )(place, *normed, right_own, right_far)


def adam_moments(rotated, first_moment, second_moment):
    first_new = beta_one * first_moment + (1.0 - beta_one) * rotated
    second_new = beta_two * second_moment + (1.0 - beta_two) * rotated * rotated
    normed = (first_new / corr_one / (jnp.sqrt(second_new / corr_two) + eps_value)).astype(
        jnp.bfloat16
    )
    return (first_new, second_new, normed)


def body(grad, left_basis, right_basis, first_moment, second_moment):
    f32, bf16 = jnp.float32, jnp.bfloat16
    y, zh, core = lax.axis_index("y"), lax.axis_index("zh"), lax.axis_index("core")
    zl, x = lax.axis_index("zl"), lax.axis_index("x")
    z = zh * 4 + zl
    rows, cols = grad.shape
    lead, part = left_basis.shape[1], left_basis.shape[1] // 4

    place = jnp.stack([x, y, zl, core]).astype(jnp.int32)

    half = rows // 2
    up1, down1 = shift(grad, RING, 8, 1), shift(grad, RING, 8, -1)
    quarters = left_basis.T.reshape(4, part, rows)
    own = [pick(quarters, zl)]
    for d in (1, 2, 3):
        own.append(shift(pick(quarters, (zl + d) % 4), "zl", 4, d))
    turned = jnp.zeros((4, part, rows), bf16)
    for d in range(4):
        turned = lax.dynamic_update_index_in_dim(turned, own[d], (zl - d) % 4, 0)
    turned = turned.reshape(4 * part, rows)
    up1, down1, turned, right_late = tie(up1, down1, turned, right_basis)

    right_own = lax.all_gather(right_late, RING).reshape(2, 4, *right_basis.shape)
    right_far = shift(right_own, "core", 2, 1)

    up2, down2 = shift(up1, RING, 8, 1), shift(down1, RING, 8, -1)
    pairs = []
    for zs in range(2):
        for xs in range(4):
            pairs.append((zs * 4 + xs, (xs // 2) * 4 + zs * 2 + xs % 2))
    turned = lax.ppermute(turned, ("zh", "x"), pairs)
    up2, down2, turned = tie(up2, down2, turned)
    up3, down3 = shift(up2, RING, 8, 1), shift(down2, RING, 8, -1)
    panel = jnp.zeros((4, 4 * part, rows), bf16)
    for k in range(4):
        got = shift(turned, "x", 4, k) if k else turned
        q = (x - k) % 4
        panel = lax.dynamic_update_index_in_dim(panel, got, (q % 2) * 2 + q // 2, 0)
    up3, down3, panel = tie(up3, down3, panel)
    panel = panel.reshape(2, 2, 4 * part, rows)
    far = jnp.concatenate([shift(up3[:half], RING, 8, 1), shift(down3[half:], RING, 8, -1)], axis=0)

    gradient = jnp.zeros((4, 2, rows, cols), bf16)
    blocks = ((0, grad), (1, up1), (-1, down1), (2, up2), (-2, down2), (3, up3), (-3, down3))
    for s, block in blocks + ((4, far),):
        gradient = lax.dynamic_update_slice(
            gradient, block[None, None], ((zl - s) % 4, ((z - s) % 8) // 4, 0, 0)
        )
    gradient = gradient.reshape(4, 2 * rows, cols)

    def rotate(which):
        pair = pick(panel, which)
        wide = jnp.concatenate([pair[0], pair[1]], axis=1)
        return jnp.stack([mm(wide, gradient[j], 1, 0) for j in range(4)])

    away = shift(rotate(1 - core), "core", 2, 1)
    summed = rotate(core) + away
    total = pick(summed, y)
    for d in (1, 2, 3):
        total = total + shift(pick(summed, (y + d) % 4).astype(bf16), "y", 4, d).astype(f32)
    rotated_in = total.astype(bf16)
    wide = [rotated_in] + [shift(rotated_in, "x", 4, d) for d in (1, 2, 3)]

    moments = jnp.stack([first_moment, second_moment]).reshape(2, 4, part, cols)
    moments, _ = tie(moments, away)
    near = [lax.dynamic_index_in_dim(moments, zl, 1, keepdims=False)]
    for e in (1, 2, 3):
        near.append(
            shift(lax.dynamic_index_in_dim(moments, (zl + e) % 4, 1, keepdims=False), "zl", 4, e)
        )
    near = jnp.concatenate(near, axis=2)

    rotated, *sent = turn_right(place, wide, right_own, right_far)
    for d in (1, 2, 3):
        rotated = rotated + shift(sent[d - 1], "y", 4, d).astype(f32)
    normed = adam_moments(rotated, near[0], near[1])[2]

    normed = [normed] + [shift(normed, "y", 4, d) for d in (1, 2, 3)]
    total, *sent = turn_back(place, normed, right_own, right_far)
    for d in (1, 2, 3):
        total = total + shift(sent[d - 1], "x", 4, d).astype(f32)
    back = total.astype(bf16)

    rotated = rotated.astype(bf16)
    home = jnp.zeros((4, part, cols), bf16)
    for e in range(4):
        piece = rotated[:, e * cols : (e + 1) * cols]
        if e:
            piece = shift(piece, "zl", 4, -e)
        home = lax.dynamic_update_index_in_dim(home, piece, (zl + e) % 4, 0)
    first_new, second_new, _ = adam_moments(
        home.reshape(rows, cols).astype(f32), first_moment, second_moment
    )

    full = jnp.zeros((4, 4 * part, cols), bf16)
    for d in range(4):
        piece = shift(back, "y", 4, d) if d else back
        full = lax.dynamic_update_index_in_dim(full, piece, (y - d) % 4, 0)
    mine = pick(panel, core)
    theirs = shift(pick(panel, 1 - core), "core", 2, 1)

    def unrotate(pair):
        flat = jnp.concatenate([pair[0], pair[1]], axis=1)
        return jnp.stack([mm(flat, full[j], 0, 0) for j in range(4)])

    away = shift(unrotate(theirs).astype(bf16), "core", 2, 1).astype(f32)
    summed = (unrotate(mine) + away).reshape(8, rows, cols)
    update = pick(summed, zl * 2 + zh)
    for t in (1, -1, 2, -2, 3, -3, 4):
        to = (z + t) % 8
        piece = pick(summed, (to % 4) * 2 + to // 4).astype(bf16)
        update = update + shift(piece, RING, 8, t).astype(f32)
    return (update, first_new, second_new)


def solution(mesh):
    names = ("y", "zh", "core", "zl", "x")
    fine = Mesh(mesh.devices.reshape(4, 2, 2, 4, 4), names)
    spec = P(("y", "zh", "core"), ("zl", "x"))
    return jax.shard_map(
        body, mesh=fine, in_specs=(spec,) * 5, out_specs=(spec,) * 3, check_vma=False
    )
```

```python
import jax
import jax.numpy as jnp
from jax import lax
from jax.experimental import pallas as pl
from jax.experimental.pallas import tpu as pltpu
from jax.sharding import Mesh
from jax.sharding import PartitionSpec as P

beta_one = 0.9
beta_two = 0.95
corr_one = 1.0 - 0.9**10
corr_two = 1.0 - 0.95**10
eps_value = 1e-08

RING = ("zh", "zl")


def shift(arr, axes, size, by):
    return lax.ppermute(arr, axes, [(i, (i + by) % size) for i in range(size)])


def pick(arr, index):
    return lax.dynamic_index_in_dim(arr, index, 0, keepdims=False)


def tie(*values):
    return lax.optimization_barrier(values)


def turn_right(place, wide, right_own, right_far):
    rows, cols = wide[0].shape
    part = rows // 4

    def kernel(at, w0, w1, w2, w3, own, far, mine, far1, far2, far3, held, total):
        x, y, core = at[0], at[1], at[3]

        @pl.when(pl.program_id(0) == 0)
        def _():
            for d, ref in enumerate((w0, w1, w2, w3)):
                held[lax.rem(x + 4 - d, 4)] = ref[...]

        acc = jnp.zeros((rows, cols), jnp.float32)
        for which, ref in ((core, own), (1 - core, far)):
            for h in range(2):
                acc += jnp.dot(held[2 * h + which], ref[h, 0], preferred_element_type=jnp.float32)
        total[...] = acc.reshape(4, part, cols)
        mine[...] = total[y]
        for d, ref in ((1, far1), (2, far2), (3, far3)):
            ref[...] = total[lax.rem(y + d, 4)].astype(jnp.bfloat16)

    whole = pl.BlockSpec((rows, cols), lambda e, at: (0, 0))
    block = pl.BlockSpec((2, 1, cols, cols), lambda e, at: (0, lax.rem(at[2] + 4 - e, 4), 0, 0))
    out = pl.BlockSpec((part, cols), lambda e, at: (0, e))
    return pl.pallas_call(
        kernel,
        grid_spec=pltpu.PrefetchScalarGridSpec(
            num_scalar_prefetch=1,
            grid=(4,),
            in_specs=[whole] * 4 + [block] * 2,
            out_specs=[out] * 4,
            scratch_shapes=[
                pltpu.VMEM((4, rows, cols), jnp.bfloat16),
                pltpu.VMEM((4, part, cols), jnp.float32),
            ],
        ),
        out_shape=[jax.ShapeDtypeStruct((part, 4 * cols), jnp.float32)]
        + [jax.ShapeDtypeStruct((part, 4 * cols), jnp.bfloat16)] * 3,
        compiler_params=pltpu.CompilerParams(vmem_limit_bytes=40 * 2**20),
        cost_estimate=pl.CostEstimate(
            flops=32 * rows * cols * cols, bytes_accessed=32 * cols * cols, transcendentals=0
        ),
    )(place, *wide, right_own, right_far)


def turn_left(place, panel, gradient):
    rows, cols = gradient.shape[2:]

    def kernel(at, left, right, away, mine):
        core = at[3]
        for which, ref in ((1 - core, away), (core, mine)):
            acc = jnp.zeros((rows, cols), jnp.float32)
            for h in range(2):
                acc += jnp.dot(left[which, h], right[h, 0], preferred_element_type=jnp.float32)
            ref[0] = acc

    out = pl.BlockSpec((1, rows, cols), lambda j, at: (j, 0, 0))
    return pl.pallas_call(
        kernel,
        grid_spec=pltpu.PrefetchScalarGridSpec(
            num_scalar_prefetch=1,
            grid=(4,),
            in_specs=[
                pl.BlockSpec(panel.shape, lambda j, at: (0, 0, 0, 0)),
                pl.BlockSpec((2, 1, rows, cols), lambda j, at: (0, lax.rem(at[1] + j, 4), 0, 0)),
            ],
            out_specs=[out] * 2,
        ),
        out_shape=[jax.ShapeDtypeStruct((4, rows, cols), jnp.float32)] * 2,
        compiler_params=pltpu.CompilerParams(vmem_limit_bytes=40 * 2**20),
        cost_estimate=pl.CostEstimate(
            flops=32 * rows * rows * cols, bytes_accessed=24 * rows * cols, transcendentals=0
        ),
    )(place, panel, gradient)


def turn_back(place, normed, right_own, right_far, half):
    part, long = normed[0].shape
    rows, cols = 4 * part, long // 4
    width = cols // 2

    def kernel(at, n0, n1, n2, n3, own, far, mine, far1, far2, far3, held):
        x, y, zl, core = at[0], at[1], at[2], at[3]
        h = pl.program_id(0)

        @pl.when(h == 0)
        def _():
            for d, ref in enumerate((n0, n1, n2, n3)):
                held[lax.rem(y + 4 - d, 4)] = ref[...]

        for which, ref in ((core, own), (1 - core, far)):
            acc = jnp.zeros((rows, width), jnp.float32)
            for e in range(4):
                acc += lax.dot_general(
                    held[:, :, e * cols : (e + 1) * cols].reshape(rows, cols),
                    ref[0, lax.rem(zl + 4 - e, 4)],
                    (((1,), (1,)), ((), ())),
                    preferred_element_type=jnp.float32,
                )
            slot = lax.rem(2 * h + which + 4 - x, 4)

            @pl.when(slot == 0)
            def _():
                mine[...] = acc

            for d, to in ((1, far1), (2, far2), (3, far3)):

                @pl.when(slot == d)
                def _():
                    to[...] = acc.astype(jnp.bfloat16)

    whole = pl.BlockSpec((part, long), lambda h, at: (0, 0))
    block = pl.BlockSpec((1, 4, width, cols), lambda h, at: (h, 0, half, 0))
    out = pl.BlockSpec((rows, width), lambda h, at: (0, 0))
    return pl.pallas_call(
        kernel,
        grid_spec=pltpu.PrefetchScalarGridSpec(
            num_scalar_prefetch=1,
            grid=(2,),
            in_specs=[whole] * 4 + [block] * 2,
            out_specs=[out] * 4,
            scratch_shapes=[pltpu.VMEM((4, part, long), jnp.bfloat16)],
        ),
        out_shape=[jax.ShapeDtypeStruct((rows, width), jnp.float32)]
        + [jax.ShapeDtypeStruct((rows, width), jnp.bfloat16)] * 3,
        compiler_params=pltpu.CompilerParams(vmem_limit_bytes=40 * 2**20),
        cost_estimate=pl.CostEstimate(
            flops=16 * rows * cols * cols, bytes_accessed=16 * cols * cols, transcendentals=0
        ),
    )(place, *normed, right_own, right_far)


def turn_left_back(place, panel, own, far):
    rows = panel.shape[2]
    width = own[0].shape[1]

    def kernel(at, left, o0, o1, o2, o3, f0, f1, f2, f3, near, plus, minus, most, held):
        y, zl, core, z = at[1], at[2], at[3], at[4]
        for d in range(4):
            slot = lax.rem(y + 4 - d, 4)
            held[core, slot] = (o0, o1, o2, o3)[d][...]
            held[1 - core, slot] = (f0, f1, f2, f3)[d][...]
        for t, (ref, k) in {
            3: (plus, 0), 5: (minus, 0), 4: (most, None), 1: (plus, 1), 7: (minus, 1),
            2: (near, 1), 6: (near, 2), 0: (near, 0),
        }.items():
            to = lax.rem(z + t, 8)
            acc = jnp.zeros((rows, width), jnp.float32)
            for c in range(2):
                acc += jnp.dot(
                    left[c, lax.div(to, 4)], held[c, lax.rem(to, 4)], preferred_element_type=jnp.float32
                )
            if k is None:
                ref[...] = acc.astype(ref.dtype)
            else:
                ref[k] = acc.astype(ref.dtype)

    vmem = pl.BlockSpec(memory_space=pltpu.VMEM)
    return pl.pallas_call(
        kernel,
        in_specs=[pl.BlockSpec(memory_space=pltpu.SMEM)] + [vmem] * 9,
        out_specs=[vmem] * 4,
        scratch_shapes=[pltpu.VMEM((2, 4, rows, width), jnp.bfloat16)],
        out_shape=[
            jax.ShapeDtypeStruct((3, rows, width), jnp.float32),
            jax.ShapeDtypeStruct((2, rows, width), jnp.bfloat16),
            jax.ShapeDtypeStruct((2, rows, width), jnp.bfloat16),
            jax.ShapeDtypeStruct((rows, width), jnp.bfloat16),
        ],
        compiler_params=pltpu.CompilerParams(vmem_limit_bytes=40 * 2**20),
        cost_estimate=pl.CostEstimate(
            flops=32 * rows * rows * width, bytes_accessed=32 * rows * width, transcendentals=0
        ),
    )(place, panel, *own, *far)


def adam_moments(rotated, first_moment, second_moment):
    first_new = beta_one * first_moment + (1.0 - beta_one) * rotated
    second_new = beta_two * second_moment + (1.0 - beta_two) * rotated * rotated
    normed = (first_new / corr_one / (jnp.sqrt(second_new / corr_two) + eps_value)).astype(
        jnp.bfloat16
    )
    return (first_new, second_new, normed)


def body(grad, left_basis, right_basis, first_moment, second_moment):
    f32, bf16 = jnp.float32, jnp.bfloat16
    y, zh, core = lax.axis_index("y"), lax.axis_index("zh"), lax.axis_index("core")
    zl, x = lax.axis_index("zl"), lax.axis_index("x")
    z = zh * 4 + zl
    rows, cols = grad.shape
    lead, part = left_basis.shape[1], left_basis.shape[1] // 4

    place = jnp.stack([x, y, zl, core, z]).astype(jnp.int32)

    gradient = lax.all_gather(grad, RING).reshape(2, 4, rows, cols)

    right_own = lax.all_gather(right_basis, RING).reshape(2, 4, *right_basis.shape)
    right_far = shift(right_own, "core", 2, 1)

    quarters = left_basis.T.reshape(4, part, rows)
    own = [pick(quarters, zl)]
    for d in (1, 2, 3):
        own.append(shift(pick(quarters, (zl + d) % 4), "zl", 4, d))
    turned = jnp.zeros((4, part, rows), bf16)
    for d in range(4):
        turned = lax.dynamic_update_index_in_dim(turned, own[d], (zl - d) % 4, 0)
    turned = turned.reshape(4 * part, rows)
    pairs = []
    for zs in range(2):
        for xs in range(4):
            pairs.append((zs * 4 + xs, (xs // 2) * 4 + zs * 2 + xs % 2))
    turned = lax.ppermute(turned, ("zh", "x"), pairs)
    panel = jnp.zeros((4, 4 * part, rows), bf16)
    for k in range(4):
        got = shift(turned, "x", 4, k) if k else turned
        q = (x - k) % 4
        panel = lax.dynamic_update_index_in_dim(panel, got, (q % 2) * 2 + q // 2, 0)
    panel = panel.reshape(2, 2, 4 * part, rows)

    away, mine = turn_left(place, panel, gradient)
    away = shift(away, "core", 2, 1)
    total = mine[0] + away[0]
    for d in (1, 2, 3):
        total = total + shift((mine[d] + away[d]).astype(bf16), "y", 4, d).astype(f32)
    rotated_in = total.astype(bf16)
    wide = [rotated_in] + [shift(rotated_in, "x", 4, d) for d in (1, 2, 3)]

    moments = jnp.stack([first_moment, second_moment]).reshape(2, 4, part, cols)
    moments, *wide = tie(moments, *wide)
    near = [lax.dynamic_index_in_dim(moments, zl, 1, keepdims=False)]
    for e in (1, 2, 3):
        near.append(
            shift(lax.dynamic_index_in_dim(moments, (zl + e) % 4, 1, keepdims=False), "zl", 4, e)
        )
    near = jnp.concatenate(near, axis=2)

    rotated, *sent = turn_right(place, wide, right_own, right_far)
    for d in (1, 2, 3):
        rotated = rotated + shift(sent[d - 1], "y", 4, d).astype(f32)
    normed = adam_moments(rotated, near[0], near[1])[2]

    normed = [normed] + [shift(normed, "y", 4, d) for d in (1, 2, 3)]
    flat = panel.swapaxes(2, 3)
    update = []
    for half in range(2):
        total, *sent = turn_back(place, normed, right_own, right_far, half)
        for d in (1, 2, 3):
            total = total + shift(sent[d - 1], "x", 4, d).astype(f32)
        back = total.astype(bf16)
        full = [back] + [shift(back, "y", 4, d) for d in (1, 2, 3)]
        near, plus, minus, most = turn_left_back(
            place, flat, full, [shift(piece, "core", 2, 1) for piece in full]
        )
        edge = rows // 2
        plus, minus = shift(plus, RING, 8, 1).astype(f32), shift(minus, RING, 8, -1).astype(f32)
        ahead, behind = shift(most[:edge], RING, 8, 2), shift(most[edge:], RING, 8, -2)
        ahead = jnp.pad(ahead.astype(f32), ((0, rows - edge), (0, 0)))
        behind = jnp.pad(behind.astype(f32), ((edge, 0), (0, 0)))
        ahead = shift((near[1] + plus[0] + ahead).astype(bf16), RING, 8, 2)
        behind = shift((near[2] + minus[0] + behind).astype(bf16), RING, 8, -2)
        update.append(near[0] + plus[1] + minus[1] + ahead.astype(f32) + behind.astype(f32))
    update = jnp.concatenate(update, axis=1)

    rotated, *_ = tie(rotated.astype(bf16), *normed[1:])
    home = jnp.zeros((4, part, cols), bf16)
    for e in range(4):
        piece = rotated[:, e * cols : (e + 1) * cols]
        if e:
            piece = shift(piece, "zl", 4, -e)
        home = lax.dynamic_update_index_in_dim(home, piece, (zl + e) % 4, 0)
    first_new, second_new, _ = adam_moments(
        home.reshape(rows, cols).astype(f32), first_moment, second_moment
    )

    return (update, first_new, second_new)


def solution(mesh):
    names = ("y", "zh", "core", "zl", "x")
    fine = Mesh(mesh.devices.reshape(4, 2, 2, 4, 4), names)
    spec = P(("y", "zh", "core"), ("zl", "x"))
    return jax.shard_map(
        body, mesh=fine, in_specs=(spec,) * 5, out_specs=(spec,) * 3, check_vma=False
    )
```

```python
import jax
import jax.numpy as jnp
from jax import lax
from jax.experimental import pallas as pl
from jax.experimental.pallas import tpu as pltpu
from jax.sharding import Mesh
from jax.sharding import PartitionSpec as P

beta_one = 0.9
beta_two = 0.95
corr_one = 1.0 - 0.9**10
corr_two = 1.0 - 0.95**10
eps_value = 1e-08

RING = ("zh", "zl")


def shift(arr, axes, size, by):
    return lax.ppermute(arr, axes, [(i, (i + by) % size) for i in range(size)])


def pick(arr, index):
    return lax.dynamic_index_in_dim(arr, index, 0, keepdims=False)


def tie(*values):
    return lax.optimization_barrier(values)


def turn_right(place, wide, right_own, right_far):
    rows, cols = wide[0].shape
    part = rows // 4

    def kernel(at, w0, w1, w2, w3, own, far, mine, far1, far2, far3, held, total):
        x, y, core = at[0], at[1], at[3]

        @pl.when(pl.program_id(0) == 0)
        def _():
            for d, ref in enumerate((w0, w1, w2, w3)):
                held[lax.rem(x + 4 - d, 4)] = ref[...]

        acc = jnp.zeros((rows, cols), jnp.float32)
        for which, ref in ((core, own), (1 - core, far)):
            for h in range(2):
                acc += jnp.dot(held[2 * h + which], ref[h, 0], preferred_element_type=jnp.float32)
        total[...] = acc.reshape(4, part, cols)
        mine[...] = total[y]
        for d, ref in ((1, far1), (2, far2), (3, far3)):
            ref[...] = total[lax.rem(y + d, 4)].astype(jnp.bfloat16)

    whole = pl.BlockSpec((rows, cols), lambda e, at: (0, 0))
    block = pl.BlockSpec((2, 1, cols, cols), lambda e, at: (0, lax.rem(at[2] + 4 - e, 4), 0, 0))
    out = pl.BlockSpec((part, cols), lambda e, at: (0, e))
    return pl.pallas_call(
        kernel,
        grid_spec=pltpu.PrefetchScalarGridSpec(
            num_scalar_prefetch=1,
            grid=(4,),
            in_specs=[whole] * 4 + [block] * 2,
            out_specs=[out] * 4,
            scratch_shapes=[
                pltpu.VMEM((4, rows, cols), jnp.bfloat16),
                pltpu.VMEM((4, part, cols), jnp.float32),
            ],
        ),
        out_shape=[jax.ShapeDtypeStruct((part, 4 * cols), jnp.float32)]
        + [jax.ShapeDtypeStruct((part, 4 * cols), jnp.bfloat16)] * 3,
        compiler_params=pltpu.CompilerParams(vmem_limit_bytes=40 * 2**20),
        cost_estimate=pl.CostEstimate(
            flops=32 * rows * cols * cols, bytes_accessed=32 * cols * cols, transcendentals=0
        ),
    )(place, *wide, right_own, right_far)


def turn_left(place, across, gradient, other):
    rows, cols = gradient.shape[2:]

    def kernel(at, l0, l1, l2, l3, right, out, left):
        @pl.when(pl.program_id(0) == 0)
        def _():
            for d, ref in enumerate((l0, l1, l2, l3)):
                left[lax.rem(at[0] + 4 - d, 4)] = ref[...]

        which = 1 - at[3] if other else at[3]
        acc = jnp.zeros((rows, cols), jnp.float32)
        for h in range(2):
            acc += jnp.dot(left[2 * h + which], right[h, 0], preferred_element_type=jnp.float32)
        out[0] = acc

    return pl.pallas_call(
        kernel,
        grid_spec=pltpu.PrefetchScalarGridSpec(
            num_scalar_prefetch=1,
            grid=(4,),
            in_specs=[
                *[pl.BlockSpec((rows, rows), lambda j, at: (0, 0))] * 4,
                pl.BlockSpec((2, 1, rows, cols), lambda j, at: (0, lax.rem(at[1] + j, 4), 0, 0)),
            ],
            out_specs=pl.BlockSpec((1, rows, cols), lambda j, at: (j, 0, 0)),
            scratch_shapes=[pltpu.VMEM((4, rows, rows), jnp.bfloat16)],
        ),
        out_shape=jax.ShapeDtypeStruct((4, rows, cols), jnp.float32),
        compiler_params=pltpu.CompilerParams(vmem_limit_bytes=40 * 2**20),
        cost_estimate=pl.CostEstimate(
            flops=16 * rows * rows * cols, bytes_accessed=16 * rows * cols, transcendentals=0
        ),
    )(place, *across, gradient)


def turn_back(place, normed, right_own, right_far):
    part, long = normed[0].shape
    rows, cols = 4 * part, long // 4
    width = cols // 2

    def kernel(at, n0, n1, n2, n3, own, far, *rest):
        outs, held = rest[:8], rest[8]
        x, y, zl, core = at[0], at[1], at[2], at[3]
        h = pl.program_id(0)

        @pl.when(h == 0)
        def _():
            for d, ref in enumerate((n0, n1, n2, n3)):
                held[lax.rem(y + 4 - d, 4)] = ref[...]

        for which, ref in ((core, own), (1 - core, far)):
            acc = jnp.zeros((rows, cols), jnp.float32)
            for e in range(4):
                acc += lax.dot_general(
                    held[:, :, e * cols : (e + 1) * cols].reshape(rows, cols),
                    ref[0, lax.rem(zl + 4 - e, 4)],
                    (((1,), (1,)), ((), ())),
                    preferred_element_type=jnp.float32,
                )
            slot = lax.rem(2 * h + which + 4 - x, 4)
            for d in range(4):

                @pl.when(slot == d)
                def _():
                    for half in range(2):
                        to = outs[half * 4 + d]
                        to[...] = acc[:, half * width : (half + 1) * width].astype(to.dtype)

    whole = pl.BlockSpec((part, long), lambda h, at: (0, 0))
    block = pl.BlockSpec((1, 4, cols, cols), lambda h, at: (h, 0, 0, 0))
    out = pl.BlockSpec((rows, width), lambda h, at: (0, 0))
    kinds = (jnp.float32, jnp.bfloat16, jnp.bfloat16, jnp.bfloat16) * 2
    outs = pl.pallas_call(
        kernel,
        grid_spec=pltpu.PrefetchScalarGridSpec(
            num_scalar_prefetch=1,
            grid=(2,),
            in_specs=[whole] * 4 + [block] * 2,
            out_specs=[out] * 8,
            scratch_shapes=[pltpu.VMEM((4, part, long), jnp.bfloat16)],
        ),
        out_shape=[jax.ShapeDtypeStruct((rows, width), kind) for kind in kinds],
        compiler_params=pltpu.CompilerParams(vmem_limit_bytes=40 * 2**20),
        cost_estimate=pl.CostEstimate(
            flops=32 * rows * cols * cols, bytes_accessed=32 * cols * cols, transcendentals=0
        ),
    )(place, *normed, right_own, right_far)
    return outs[:4], outs[4:]


def turn_left_back(place, across, own, far):
    rows = across[0].shape[0]
    width = own[0].shape[1]

    def kernel(at, l0, l1, l2, l3, o0, o1, o2, o3, f0, f1, f2, f3, near, plus, minus, most, held, left):
        x, y, zl, core, z = at[0], at[1], at[2], at[3], at[4]
        for d in range(4):
            slot = lax.rem(y + 4 - d, 4)
            held[core, slot] = (o0, o1, o2, o3)[d][...]
            held[1 - core, slot] = (f0, f1, f2, f3)[d][...]
            left[lax.rem(x + 4 - d, 4)] = (l0, l1, l2, l3)[d][...].T
        for t, (ref, k) in {
            3: (plus, 0), 5: (minus, 0), 4: (most, None), 1: (plus, 1), 7: (minus, 1),
            2: (near, 1), 6: (near, 2), 0: (near, 0),
        }.items():
            to = lax.rem(z + t, 8)
            acc = jnp.zeros((rows, width), jnp.float32)
            for c in range(2):
                acc += jnp.dot(
                    left[2 * lax.div(to, 4) + c], held[c, lax.rem(to, 4)], preferred_element_type=jnp.float32
                )
            if k is None:
                ref[...] = acc.astype(ref.dtype)
            else:
                ref[k] = acc.astype(ref.dtype)

    vmem = pl.BlockSpec(memory_space=pltpu.VMEM)
    return pl.pallas_call(
        kernel,
        in_specs=[pl.BlockSpec(memory_space=pltpu.SMEM)] + [vmem] * 12,
        out_specs=[vmem] * 4,
        scratch_shapes=[
            pltpu.VMEM((2, 4, rows, width), jnp.bfloat16),
            pltpu.VMEM((4, rows, rows), jnp.bfloat16),
        ],
        out_shape=[
            jax.ShapeDtypeStruct((3, rows, width), jnp.float32),
            jax.ShapeDtypeStruct((2, rows, width), jnp.bfloat16),
            jax.ShapeDtypeStruct((2, rows, width), jnp.bfloat16),
            jax.ShapeDtypeStruct((rows, width), jnp.bfloat16),
        ],
        compiler_params=pltpu.CompilerParams(vmem_limit_bytes=40 * 2**20),
        cost_estimate=pl.CostEstimate(
            flops=32 * rows * rows * width, bytes_accessed=32 * rows * width, transcendentals=0
        ),
    )(place, *across, *own, *far)


def adam_moments(rotated, first_moment, second_moment):
    first_new = beta_one * first_moment + (1.0 - beta_one) * rotated
    second_new = beta_two * second_moment + (1.0 - beta_two) * rotated * rotated
    normed = (first_new / corr_one / (jnp.sqrt(second_new / corr_two) + eps_value)).astype(
        jnp.bfloat16
    )
    return (first_new, second_new, normed)


def body(grad, left_basis, right_basis, first_moment, second_moment):
    f32, bf16 = jnp.float32, jnp.bfloat16
    y, zh, core = lax.axis_index("y"), lax.axis_index("zh"), lax.axis_index("core")
    zl, x = lax.axis_index("zl"), lax.axis_index("x")
    z = zh * 4 + zl
    rows, cols = grad.shape
    lead, part = left_basis.shape[1], left_basis.shape[1] // 4

    place = jnp.stack([x, y, zl, core, z]).astype(jnp.int32)

    up1, down1 = shift(grad, RING, 8, 1), shift(grad, RING, 8, -1)
    quarters = left_basis.T.reshape(4, part, rows)
    got = []
    for d in range(4):
        pairs = []
        for zs in range(2):
            for ls in range(4):
                for xs in range(4):
                    to = ((xs // 2) * 4 + (ls + d) % 4) * 4 + zs * 2 + xs % 2
                    pairs.append(((zs * 4 + ls) * 4 + xs, to))
        got.append(lax.ppermute(pick(quarters, (zl + d) % 4), ("zh", "zl", "x"), pairs))
    up1, down1 = tie(up1, down1)

    up2, down2 = shift(up1, RING, 8, 1), shift(down1, RING, 8, -1)
    up2, down2, g0, g1, g2, g3 = tie(up2, down2, *got)
    turned = jnp.zeros((4, part, rows), bf16)
    for d, piece in enumerate((g0, g1, g2, g3)):
        turned = lax.dynamic_update_index_in_dim(turned, piece, (zl - d) % 4, 0)
    turned = turned.reshape(4 * part, rows)
    up3, down3 = shift(up2, RING, 8, 1), shift(down2, RING, 8, -1)
    across = [turned] + [shift(turned, "x", 4, k) for k in (1, 2, 3)]
    half = rows // 2
    up4, down4 = shift(up3[:half], RING, 8, 1), shift(down3[half:], RING, 8, -1)

    right_late, _, _ = tie(right_basis, up3, down3)
    right_own = lax.all_gather(right_late, RING).reshape(2, 4, *right_basis.shape)

    gradient = jnp.zeros((8, rows, cols), bf16)
    blocks = ((0, grad), (1, up1), (-1, down1), (2, up2), (-2, down2), (3, up3), (-3, down3))
    for s, block in blocks:
        gradient = lax.dynamic_update_index_in_dim(gradient, block, (z - s) % 8, 0)
    gradient = lax.dynamic_update_slice(gradient, up4[None], ((z + 4) % 8, 0, 0))
    gradient = lax.dynamic_update_slice(gradient, down4[None], ((z + 4) % 8, half, 0))
    gradient = gradient.reshape(2, 4, rows, cols)

    away = shift(turn_left(place, across, gradient, True), "core", 2, 1)
    mine = turn_left(place, across, gradient, False)
    total = mine[0] + away[0]
    for d in (1, 2, 3):
        total = total + shift((mine[d] + away[d]).astype(bf16), "y", 4, d).astype(f32)
    rotated_in = total.astype(bf16)
    wide = [rotated_in] + [shift(rotated_in, "x", 4, d) for d in (1, 2, 3)]
    right_own, _ = tie(right_own, wide[1])
    right_far = shift(right_own, "core", 2, 1)
    moments, _ = tie(jnp.stack([first_moment, second_moment]), right_own)

    moments = moments.reshape(2, 4, part, cols)
    near = [lax.dynamic_index_in_dim(moments, zl, 1, keepdims=False)]
    for e in (1, 2, 3):
        near.append(
            shift(lax.dynamic_index_in_dim(moments, (zl + e) % 4, 1, keepdims=False), "zl", 4, e)
        )
    near = jnp.concatenate(near, axis=2)

    rotated, *sent = turn_right(place, wide, right_own, right_far)
    for d in (1, 2, 3):
        rotated = rotated + shift(sent[d - 1], "y", 4, d).astype(f32)
    normed = adam_moments(rotated, near[0], near[1])[2]

    normed, late = tie(normed, rotated.astype(bf16))
    normed = [normed] + [shift(normed, "y", 4, d) for d in (1, 2, 3)]
    pieces = [late[:, e * cols : (e + 1) * cols] for e in range(4)]
    pieces = [pieces[0]] + [shift(pieces[e], "zl", 4, -e) for e in (1, 2, 3)]
    *normed, p0, p1, p2, p3 = tie(*normed, *pieces)

    first, second = turn_back(place, normed, right_own, right_far)
    *second, p0, p1, p2, p3 = tie(*second, p0, p1, p2, p3)
    home = jnp.zeros((4, part, cols), bf16)
    for e, piece in enumerate((p0, p1, p2, p3)):
        home = lax.dynamic_update_index_in_dim(home, piece, (zl + e) % 4, 0)
    first_new, second_new, _ = adam_moments(
        home.reshape(rows, cols).astype(f32), first_moment, second_moment
    )
    update = []
    for total, *sent in (first, second):
        for d in (1, 2, 3):
            total = total + shift(sent[d - 1], "x", 4, d).astype(f32)
        back = total.astype(bf16)
        full = [back] + [shift(back, "y", 4, d) for d in (1, 2, 3)]
        near, plus, minus, most = turn_left_back(
            place, across, full, [shift(piece, "core", 2, 1) for piece in full]
        )
        edge = rows // 2
        plus, minus = shift(plus, RING, 8, 1).astype(f32), shift(minus, RING, 8, -1).astype(f32)
        ahead, behind = shift(most[:edge], RING, 8, 2), shift(most[edge:], RING, 8, -2)
        ahead = jnp.pad(ahead.astype(f32), ((0, rows - edge), (0, 0)))
        behind = jnp.pad(behind.astype(f32), ((edge, 0), (0, 0)))
        ahead = shift((near[1] + plus[0] + ahead).astype(bf16), RING, 8, 2)
        behind = shift((near[2] + minus[0] + behind).astype(bf16), RING, 8, -2)
        update.append(near[0] + plus[1] + minus[1] + ahead.astype(f32) + behind.astype(f32))
    update = jnp.concatenate(update, axis=1)

    return (update, first_new, second_new)


def solution(mesh):
    names = ("y", "zh", "core", "zl", "x")
    fine = Mesh(mesh.devices.reshape(4, 2, 2, 4, 4), names)
    spec = P(("y", "zh", "core"), ("zl", "x"))
    return jax.shard_map(
        body, mesh=fine, in_specs=(spec,) * 5, out_specs=(spec,) * 3, check_vma=False
    )
```

```python
import jax
import jax.numpy as jnp
from jax import lax
from jax.experimental import pallas as pl
from jax.experimental.pallas import tpu as pltpu
from jax.sharding import Mesh
from jax.sharding import PartitionSpec as P

beta_one = 0.9
beta_two = 0.95
corr_one = 1.0 - 0.9**10
corr_two = 1.0 - 0.95**10
eps_value = 1e-08

RING = ("zh", "zl")


def shift(arr, axes, size, by):
    return lax.ppermute(arr, axes, [(i, (i + by) % size) for i in range(size)])


def split_ways(arr, by):
    pairs = []
    for core in range(2):
        for z in range(8):
            to = (z + (by, -by)[core]) % 8
            pairs.append(((z // 4 * 2 + core) * 4 + z % 4, (to // 4 * 2 + core) * 4 + to % 4))
    return lax.ppermute(arr, ("zh", "core", "zl"), pairs)


def pick(arr, index):
    return lax.dynamic_index_in_dim(arr, index, 0, keepdims=False)


def tie(*values):
    return lax.optimization_barrier(values)


def turn_right(place, wide, right_own, right_far):
    rows, cols = wide[0].shape
    part = rows // 4

    def kernel(at, w0, w1, w2, w3, own, far, mine, far1, far2, far3, held, total):
        x, y, core = at[0], at[1], at[3]

        @pl.when(pl.program_id(0) == 0)
        def _():
            for d, ref in enumerate((w0, w1, w2, w3)):
                held[lax.rem(x + 4 - d, 4)] = ref[...]

        acc = jnp.zeros((rows, cols), jnp.float32)
        for which, ref in ((core, own), (1 - core, far)):
            for h in range(2):
                acc += jnp.dot(held[2 * h + which], ref[h, 0], preferred_element_type=jnp.float32)
        total[...] = acc.reshape(4, part, cols)
        mine[...] = total[y]
        for d, ref in ((1, far1), (2, far2), (3, far3)):
            ref[...] = total[lax.rem(y + d, 4)].astype(jnp.bfloat16)

    whole = pl.BlockSpec((rows, cols), lambda e, at: (0, 0))
    block = pl.BlockSpec((2, 1, cols, cols), lambda e, at: (0, lax.rem(at[2] + 4 - e, 4), 0, 0))
    out = pl.BlockSpec((part, cols), lambda e, at: (0, e))
    return pl.pallas_call(
        kernel,
        grid_spec=pltpu.PrefetchScalarGridSpec(
            num_scalar_prefetch=1,
            grid=(4,),
            in_specs=[whole] * 4 + [block] * 2,
            out_specs=[out] * 4,
            scratch_shapes=[
                pltpu.VMEM((4, rows, cols), jnp.bfloat16),
                pltpu.VMEM((4, part, cols), jnp.float32),
            ],
        ),
        out_shape=[jax.ShapeDtypeStruct((part, 4 * cols), jnp.float32)]
        + [jax.ShapeDtypeStruct((part, 4 * cols), jnp.bfloat16)] * 3,
        compiler_params=pltpu.CompilerParams(vmem_limit_bytes=40 * 2**20),
        cost_estimate=pl.CostEstimate(
            flops=32 * rows * cols * cols, bytes_accessed=32 * cols * cols, transcendentals=0
        ),
    )(place, *wide, right_own, right_far)


def turn_left(place, across, gradient, other):
    rows, cols = gradient.shape[2:]

    def kernel(at, l0, l1, l2, l3, right, out, left):
        @pl.when(pl.program_id(0) == 0)
        def _():
            for d, ref in enumerate((l0, l1, l2, l3)):
                left[lax.rem(at[0] + 4 - d, 4)] = ref[...]

        which = 1 - at[3] if other else at[3]
        acc = jnp.zeros((rows, cols), jnp.float32)
        for h in range(2):
            acc += jnp.dot(left[2 * h + which], right[h, 0], preferred_element_type=jnp.float32)
        out[0] = acc

    return pl.pallas_call(
        kernel,
        grid_spec=pltpu.PrefetchScalarGridSpec(
            num_scalar_prefetch=1,
            grid=(4,),
            in_specs=[
                *[pl.BlockSpec((rows, rows), lambda j, at: (0, 0))] * 4,
                pl.BlockSpec((2, 1, rows, cols), lambda j, at: (0, lax.rem(at[1] + j, 4), 0, 0)),
            ],
            out_specs=pl.BlockSpec((1, rows, cols), lambda j, at: (j, 0, 0)),
            scratch_shapes=[pltpu.VMEM((4, rows, rows), jnp.bfloat16)],
        ),
        out_shape=jax.ShapeDtypeStruct((4, rows, cols), jnp.float32),
        compiler_params=pltpu.CompilerParams(vmem_limit_bytes=40 * 2**20),
        cost_estimate=pl.CostEstimate(
            flops=16 * rows * rows * cols, bytes_accessed=16 * rows * cols, transcendentals=0
        ),
    )(place, *across, gradient)


def turn_back(place, normed, right_own, right_far):
    part, long = normed[0].shape
    rows, cols = 4 * part, long // 4
    width = cols // 2

    def kernel(at, n0, n1, n2, n3, own, far, *rest):
        outs, held = rest[:8], rest[8]
        x, y, zl, core = at[0], at[1], at[2], at[3]
        h = pl.program_id(0)

        @pl.when(h == 0)
        def _():
            for d, ref in enumerate((n0, n1, n2, n3)):
                held[lax.rem(y + 4 - d, 4)] = ref[...]

        for which, ref in ((core, own), (1 - core, far)):
            acc = jnp.zeros((rows, cols), jnp.float32)
            for e in range(4):
                acc += lax.dot_general(
                    held[:, :, e * cols : (e + 1) * cols].reshape(rows, cols),
                    ref[0, lax.rem(zl + 4 - e, 4)],
                    (((1,), (1,)), ((), ())),
                    preferred_element_type=jnp.float32,
                )
            slot = lax.rem(2 * h + which + 4 - x, 4)
            for d in range(4):

                @pl.when(slot == d)
                def _():
                    for half in range(2):
                        to = outs[half * 4 + d]
                        to[...] = acc[:, half * width : (half + 1) * width].astype(to.dtype)

    whole = pl.BlockSpec((part, long), lambda h, at: (0, 0))
    block = pl.BlockSpec((1, 4, cols, cols), lambda h, at: (h, 0, 0, 0))
    out = pl.BlockSpec((rows, width), lambda h, at: (0, 0))
    kinds = (jnp.float32, jnp.bfloat16, jnp.bfloat16, jnp.bfloat16) * 2
    outs = pl.pallas_call(
        kernel,
        grid_spec=pltpu.PrefetchScalarGridSpec(
            num_scalar_prefetch=1,
            grid=(2,),
            in_specs=[whole] * 4 + [block] * 2,
            out_specs=[out] * 8,
            scratch_shapes=[pltpu.VMEM((4, part, long), jnp.bfloat16)],
        ),
        out_shape=[jax.ShapeDtypeStruct((rows, width), kind) for kind in kinds],
        compiler_params=pltpu.CompilerParams(vmem_limit_bytes=40 * 2**20),
        cost_estimate=pl.CostEstimate(
            flops=32 * rows * cols * cols, bytes_accessed=32 * cols * cols, transcendentals=0
        ),
    )(place, *normed, right_own, right_far)
    return outs[:4], outs[4:]


def turn_left_back(place, across, own, far):
    rows = across[0].shape[0]
    width = own[0].shape[1]

    def kernel(at, l0, l1, l2, l3, o0, o1, o2, o3, other, near, plus, minus, most, held, left):
        x, y, zl, core, z = at[0], at[1], at[2], at[3], at[4]
        for d in range(4):
            slot = lax.rem(y + 4 - d, 4)
            held[core, slot] = (o0, o1, o2, o3)[d][...]
            held[1 - core, slot] = other[d]
            left[lax.rem(x + 4 - d, 4)] = (l0, l1, l2, l3)[d][...].T
        for t, (ref, k) in {
            3: (plus, 0), 5: (minus, 0), 4: (most, None), 1: (plus, 1), 7: (minus, 1),
            2: (near, 1), 6: (near, 2), 0: (near, 0),
        }.items():
            to = lax.rem(z + t, 8)
            acc = jnp.zeros((rows, width), jnp.float32)
            for c in range(2):
                acc += jnp.dot(
                    left[2 * lax.div(to, 4) + c], held[c, lax.rem(to, 4)], preferred_element_type=jnp.float32
                )
            if k is None:
                ref[...] = acc.astype(ref.dtype)
            else:
                ref[k] = acc.astype(ref.dtype)

    vmem = pl.BlockSpec(memory_space=pltpu.VMEM)
    return pl.pallas_call(
        kernel,
        in_specs=[pl.BlockSpec(memory_space=pltpu.SMEM)] + [vmem] * 9,
        out_specs=[vmem] * 4,
        scratch_shapes=[
            pltpu.VMEM((2, 4, rows, width), jnp.bfloat16),
            pltpu.VMEM((4, rows, rows), jnp.bfloat16),
        ],
        out_shape=[
            jax.ShapeDtypeStruct((3, rows, width), jnp.float32),
            jax.ShapeDtypeStruct((2, rows, width), jnp.bfloat16),
            jax.ShapeDtypeStruct((2, rows, width), jnp.bfloat16),
            jax.ShapeDtypeStruct((rows, width), jnp.bfloat16),
        ],
        compiler_params=pltpu.CompilerParams(vmem_limit_bytes=40 * 2**20),
        cost_estimate=pl.CostEstimate(
            flops=32 * rows * rows * width, bytes_accessed=32 * rows * width, transcendentals=0
        ),
    )(place, *across, *own, far)


def adam_moments(rotated, first_moment, second_moment):
    first_new = beta_one * first_moment + (1.0 - beta_one) * rotated
    second_new = beta_two * second_moment + (1.0 - beta_two) * rotated * rotated
    normed = (first_new / corr_one / (jnp.sqrt(second_new / corr_two) + eps_value)).astype(
        jnp.bfloat16
    )
    return (first_new, second_new, normed)


def body(grad, left_basis, right_basis, first_moment, second_moment):
    f32, bf16 = jnp.float32, jnp.bfloat16
    y, zh, core = lax.axis_index("y"), lax.axis_index("zh"), lax.axis_index("core")
    zl, x = lax.axis_index("zl"), lax.axis_index("x")
    z = zh * 4 + zl
    rows, cols = grad.shape
    lead, part = left_basis.shape[1], left_basis.shape[1] // 4

    place = jnp.stack([x, y, zl, core, z]).astype(jnp.int32)

    up1, down1 = shift(grad, RING, 8, 1), shift(grad, RING, 8, -1)
    quarters = left_basis.T.reshape(4, part, rows)
    got = []
    for d in range(4):
        pairs = []
        for zs in range(2):
            for ls in range(4):
                for xs in range(4):
                    to = ((xs // 2) * 4 + (ls + d) % 4) * 4 + zs * 2 + xs % 2
                    pairs.append(((zs * 4 + ls) * 4 + xs, to))
        got.append(lax.ppermute(pick(quarters, (zl + d) % 4), ("zh", "zl", "x"), pairs))
    up1, down1, g0, g1, g2, g3 = tie(up1, down1, *got)

    up2, down2 = shift(up1, RING, 8, 1), shift(down1, RING, 8, -1)
    turned = jnp.zeros((4, part, rows), bf16)
    for d, piece in enumerate((g0, g1, g2, g3)):
        turned = lax.dynamic_update_index_in_dim(turned, piece, (zl - d) % 4, 0)
    turned = turned.reshape(4 * part, rows)
    across = [turned] + [shift(turned, "x", 4, k) for k in (1, 2, 3)]
    up3, down3 = shift(up2, RING, 8, 1), shift(down2, RING, 8, -1)
    up3, down3, *across = tie(up3, down3, *across)
    half = rows // 2
    up4, down4 = shift(up3[:half], RING, 8, 1), shift(down3[half:], RING, 8, -1)

    right_late, _, _ = tie(right_basis, up3, down3)
    right_own = lax.all_gather(right_late, RING).reshape(2, 4, *right_basis.shape)

    gradient = jnp.zeros((8, rows, cols), bf16)
    blocks = ((0, grad), (1, up1), (-1, down1), (2, up2), (-2, down2), (3, up3), (-3, down3))
    for s, block in blocks:
        gradient = lax.dynamic_update_index_in_dim(gradient, block, (z - s) % 8, 0)
    gradient = lax.dynamic_update_slice(gradient, up4[None], ((z + 4) % 8, 0, 0))
    gradient = lax.dynamic_update_slice(gradient, down4[None], ((z + 4) % 8, half, 0))
    gradient = gradient.reshape(2, 4, rows, cols)

    away = shift(turn_left(place, across, gradient, True), "core", 2, 1)
    mine = turn_left(place, across, gradient, False)
    total = mine[0] + away[0]
    for d in (1, 2, 3):
        total = total + shift((mine[d] + away[d]).astype(bf16), "y", 4, d).astype(f32)
    rotated_in = total.astype(bf16)
    wide = [rotated_in] + [shift(rotated_in, "x", 4, d) for d in (1, 2, 3)]
    right_own, *_ = tie(right_own, *wide)
    right_far = shift(right_own, "core", 2, 1)
    moments, _ = tie(jnp.stack([first_moment, second_moment]), rotated_in)

    moments = moments.reshape(2, 4, part, cols)
    near = [lax.dynamic_index_in_dim(moments, zl, 1, keepdims=False)]
    for e in (1, 2, 3):
        near.append(
            shift(lax.dynamic_index_in_dim(moments, (zl + e) % 4, 1, keepdims=False), "zl", 4, e)
        )
    near = jnp.concatenate(near, axis=2)

    rotated, *sent = turn_right(place, wide, right_own, right_far)
    for d in (1, 2, 3):
        rotated = rotated + shift(sent[d - 1], "y", 4, d).astype(f32)
    normed = adam_moments(rotated, near[0], near[1])[2]

    normed, late = tie(normed, rotated.astype(bf16))
    normed = [normed] + [shift(normed, "y", 4, d) for d in (1, 2, 3)]
    pieces = [late[:, e * cols : (e + 1) * cols] for e in range(4)]
    pieces = [pieces[0]] + [shift(pieces[e], "zl", 4, -e) for e in (1, 2, 3)]
    *normed, p0, p1, p2, p3 = tie(*normed, *pieces)

    early, later = turn_back(place, normed, right_own, right_far)
    *later, p0, p1, p2, p3 = tie(*later, p0, p1, p2, p3)
    home = jnp.zeros((4, part, cols), bf16)
    for e, piece in enumerate((p0, p1, p2, p3)):
        home = lax.dynamic_update_index_in_dim(home, piece, (zl + e) % 4, 0)
    first_new, second_new, _ = adam_moments(
        home.reshape(rows, cols).astype(f32), first_moment, second_moment
    )
    update = []
    for total, *sent in (early, later):
        for d in (1, 2, 3):
            total = total + shift(sent[d - 1], "x", 4, d).astype(f32)
        back = total.astype(bf16)
        full = [back] + [shift(back, "y", 4, d) for d in (1, 2, 3)]
        near, plus, minus, most = turn_left_back(
            place, across, full, shift(jnp.stack(full), "core", 2, 1)
        )
        plus, minus = shift(plus, RING, 8, 1).astype(f32), shift(minus, RING, 8, -1).astype(f32)
        most = split_ways(most, 2).astype(f32)
        ahead, behind = jnp.where(core == 0, most, 0.0), jnp.where(core == 0, 0.0, most)
        ahead = shift((near[1] + plus[0] + ahead).astype(bf16), RING, 8, 2)
        behind = shift((near[2] + minus[0] + behind).astype(bf16), RING, 8, -2)
        update.append(near[0] + plus[1] + minus[1] + ahead.astype(f32) + behind.astype(f32))
    update = jnp.concatenate(update, axis=1)

    return (update, first_new, second_new)


def solution(mesh):
    names = ("y", "zh", "core", "zl", "x")
    fine = Mesh(mesh.devices.reshape(4, 2, 2, 4, 4), names)
    spec = P(("y", "zh", "core"), ("zl", "x"))
    return jax.shard_map(
        body, mesh=fine, in_specs=(spec,) * 5, out_specs=(spec,) * 3, check_vma=False
    )
```

```python
import jax
import jax.numpy as jnp
from jax import lax
from jax.experimental import pallas as pl
from jax.experimental.pallas import tpu as pltpu
from jax.sharding import Mesh
from jax.sharding import PartitionSpec as P

beta_one = 0.9
beta_two = 0.95
corr_one = 1.0 - 0.9**10
corr_two = 1.0 - 0.95**10
eps_value = 1e-08

RING = ("zh", "zl")


def shift(arr, axes, size, by):
    return lax.ppermute(arr, axes, [(i, (i + by) % size) for i in range(size)])


def split_ways(arr, by):
    pairs = []
    for core in range(2):
        for z in range(8):
            to = (z + (by, -by)[core]) % 8
            pairs.append(((z // 4 * 2 + core) * 4 + z % 4, (to // 4 * 2 + core) * 4 + to % 4))
    return lax.ppermute(arr, ("zh", "core", "zl"), pairs)


def pick(arr, index):
    return lax.dynamic_index_in_dim(arr, index, 0, keepdims=False)


def tie(*values):
    return lax.optimization_barrier(values)


def turn_right(place, wide, right_own, right_far):
    rows, cols = wide[0].shape
    part = rows // 4

    def kernel(at, w0, w1, w2, w3, own, far, mine, far1, far2, far3, held, total):
        x, y, core = at[0], at[1], at[3]

        @pl.when(pl.program_id(0) == 0)
        def _():
            for d, ref in enumerate((w0, w1, w2, w3)):
                held[lax.rem(x + 4 - d, 4)] = ref[...]

        acc = jnp.zeros((rows, cols), jnp.float32)
        for which, ref in ((core, own), (1 - core, far)):
            for h in range(2):
                acc += jnp.dot(held[2 * h + which], ref[h, 0], preferred_element_type=jnp.float32)
        total[...] = acc.reshape(4, part, cols)
        mine[...] = total[y]
        for d, ref in ((1, far1), (2, far2), (3, far3)):
            ref[...] = total[lax.rem(y + d, 4)].astype(jnp.bfloat16)

    whole = pl.BlockSpec((rows, cols), lambda e, at: (0, 0))
    block = pl.BlockSpec((2, 1, cols, cols), lambda e, at: (0, lax.rem(at[2] + 4 - e, 4), 0, 0))
    out = pl.BlockSpec((part, cols), lambda e, at: (0, e))
    return pl.pallas_call(
        kernel,
        grid_spec=pltpu.PrefetchScalarGridSpec(
            num_scalar_prefetch=1,
            grid=(4,),
            in_specs=[whole] * 4 + [block] * 2,
            out_specs=[out] * 4,
            scratch_shapes=[
                pltpu.VMEM((4, rows, cols), jnp.bfloat16),
                pltpu.VMEM((4, part, cols), jnp.float32),
            ],
        ),
        out_shape=[jax.ShapeDtypeStruct((part, 4 * cols), jnp.float32)]
        + [jax.ShapeDtypeStruct((part, 4 * cols), jnp.bfloat16)] * 3,
        compiler_params=pltpu.CompilerParams(vmem_limit_bytes=40 * 2**20),
        cost_estimate=pl.CostEstimate(
            flops=32 * rows * cols * cols, bytes_accessed=32 * cols * cols, transcendentals=0
        ),
    )(place, *wide, right_own, right_far)


def turn_left(place, across, gradient, other):
    rows, cols = gradient.shape[2:]

    def kernel(at, l0, l1, l2, l3, right, out, left):
        @pl.when(pl.program_id(0) == 0)
        def _():
            for d, ref in enumerate((l0, l1, l2, l3)):
                left[lax.rem(at[0] + 4 - d, 4)] = ref[...]

        which = 1 - at[3] if other else at[3]
        acc = jnp.zeros((rows, cols), jnp.float32)
        for h in range(2):
            acc += jnp.dot(left[2 * h + which], right[h, 0], preferred_element_type=jnp.float32)
        out[0] = acc

    return pl.pallas_call(
        kernel,
        grid_spec=pltpu.PrefetchScalarGridSpec(
            num_scalar_prefetch=1,
            grid=(4,),
            in_specs=[
                *[pl.BlockSpec((rows, rows), lambda j, at: (0, 0))] * 4,
                pl.BlockSpec((2, 1, rows, cols), lambda j, at: (0, lax.rem(at[1] + j, 4), 0, 0)),
            ],
            out_specs=pl.BlockSpec((1, rows, cols), lambda j, at: (j, 0, 0)),
            scratch_shapes=[pltpu.VMEM((4, rows, rows), jnp.bfloat16)],
        ),
        out_shape=jax.ShapeDtypeStruct((4, rows, cols), jnp.float32),
        compiler_params=pltpu.CompilerParams(vmem_limit_bytes=40 * 2**20),
        cost_estimate=pl.CostEstimate(
            flops=16 * rows * rows * cols, bytes_accessed=16 * rows * cols, transcendentals=0
        ),
    )(place, *across, gradient)


def turn_back(place, normed, right_own, right_far):
    part, long = normed[0].shape
    rows, cols = 4 * part, long // 4
    width = cols // 2

    def kernel(at, n0, n1, n2, n3, own, far, *rest):
        outs, held = rest[:8], rest[8]
        x, y, zl, core = at[0], at[1], at[2], at[3]
        h = pl.program_id(0)

        @pl.when(h == 0)
        def _():
            for d, ref in enumerate((n0, n1, n2, n3)):
                held[lax.rem(y + 4 - d, 4)] = ref[...]

        for which, ref in ((core, own), (1 - core, far)):
            acc = jnp.zeros((rows, cols), jnp.float32)
            for e in range(4):
                acc += lax.dot_general(
                    held[:, :, e * cols : (e + 1) * cols].reshape(rows, cols),
                    ref[0, lax.rem(zl + 4 - e, 4)],
                    (((1,), (1,)), ((), ())),
                    preferred_element_type=jnp.float32,
                )
            slot = lax.rem(2 * h + which + 4 - x, 4)
            for d in range(4):

                @pl.when(slot == d)
                def _():
                    for half in range(2):
                        to = outs[half * 4 + d]
                        to[...] = acc[:, half * width : (half + 1) * width].astype(to.dtype)

    whole = pl.BlockSpec((part, long), lambda h, at: (0, 0))
    block = pl.BlockSpec((1, 4, cols, cols), lambda h, at: (h, 0, 0, 0))
    out = pl.BlockSpec((rows, width), lambda h, at: (0, 0))
    kinds = (jnp.float32, jnp.bfloat16, jnp.bfloat16, jnp.bfloat16) * 2
    outs = pl.pallas_call(
        kernel,
        grid_spec=pltpu.PrefetchScalarGridSpec(
            num_scalar_prefetch=1,
            grid=(2,),
            in_specs=[whole] * 4 + [block] * 2,
            out_specs=[out] * 8,
            scratch_shapes=[pltpu.VMEM((4, part, long), jnp.bfloat16)],
        ),
        out_shape=[jax.ShapeDtypeStruct((rows, width), kind) for kind in kinds],
        compiler_params=pltpu.CompilerParams(vmem_limit_bytes=40 * 2**20),
        cost_estimate=pl.CostEstimate(
            flops=32 * rows * cols * cols, bytes_accessed=32 * cols * cols, transcendentals=0
        ),
    )(place, *normed, right_own, right_far)
    return outs[:4], outs[4:]


def turn_left_back(place, across, own, far):
    rows = across[0].shape[0]
    width = own[0].shape[1]

    def kernel(at, l0, l1, l2, l3, o0, o1, o2, o3, other, near, plus, minus, most, held, left):
        x, y, zl, core, z = at[0], at[1], at[2], at[3], at[4]
        for d in range(4):
            slot = lax.rem(y + 4 - d, 4)
            held[core, slot] = (o0, o1, o2, o3)[d][...]
            held[1 - core, slot] = other[d]
            left[lax.rem(x + 4 - d, 4)] = (l0, l1, l2, l3)[d][...].T
        for t, (ref, k) in {
            3: (plus, 0), 5: (minus, 0), 4: (most, None), 1: (plus, 1), 7: (minus, 1),
            2: (near, 1), 6: (near, 2), 0: (near, 0),
        }.items():
            to = lax.rem(z + t, 8)
            acc = jnp.zeros((rows, width), jnp.float32)
            for c in range(2):
                acc += jnp.dot(
                    left[2 * lax.div(to, 4) + c], held[c, lax.rem(to, 4)], preferred_element_type=jnp.float32
                )
            if k is None:
                ref[...] = acc.astype(ref.dtype)
            else:
                ref[k] = acc.astype(ref.dtype)

    vmem = pl.BlockSpec(memory_space=pltpu.VMEM)
    return pl.pallas_call(
        kernel,
        in_specs=[pl.BlockSpec(memory_space=pltpu.SMEM)] + [vmem] * 9,
        out_specs=[vmem] * 4,
        scratch_shapes=[
            pltpu.VMEM((2, 4, rows, width), jnp.bfloat16),
            pltpu.VMEM((4, rows, rows), jnp.bfloat16),
        ],
        out_shape=[
            jax.ShapeDtypeStruct((3, rows, width), jnp.float32),
            jax.ShapeDtypeStruct((2, rows, width), jnp.bfloat16),
            jax.ShapeDtypeStruct((2, rows, width), jnp.bfloat16),
            jax.ShapeDtypeStruct((rows, width), jnp.bfloat16),
        ],
        compiler_params=pltpu.CompilerParams(vmem_limit_bytes=40 * 2**20),
        cost_estimate=pl.CostEstimate(
            flops=32 * rows * rows * width, bytes_accessed=32 * rows * width, transcendentals=0
        ),
    )(place, *across, *own, far)


def adam_moments(rotated, first_moment, second_moment):
    first_new = beta_one * first_moment + (1.0 - beta_one) * rotated
    second_new = beta_two * second_moment + (1.0 - beta_two) * rotated * rotated
    normed = (first_new / corr_one / (jnp.sqrt(second_new / corr_two) + eps_value)).astype(
        jnp.bfloat16
    )
    return (first_new, second_new, normed)


def body(grad, left_basis, right_basis, first_moment, second_moment):
    f32, bf16 = jnp.float32, jnp.bfloat16
    y, zh, core = lax.axis_index("y"), lax.axis_index("zh"), lax.axis_index("core")
    zl, x = lax.axis_index("zl"), lax.axis_index("x")
    z = zh * 4 + zl
    rows, cols = grad.shape
    lead, part = left_basis.shape[1], left_basis.shape[1] // 4

    place = jnp.stack([x, y, zl, core, z]).astype(jnp.int32)

    up1, down1 = shift(grad, RING, 8, 1), shift(grad, RING, 8, -1)
    quarters = left_basis.T.reshape(4, part, rows)
    got = []
    for d in range(4):
        pairs = []
        for zs in range(2):
            for ls in range(4):
                for xs in range(4):
                    to = ((xs // 2) * 4 + (ls + d) % 4) * 4 + zs * 2 + xs % 2
                    pairs.append(((zs * 4 + ls) * 4 + xs, to))
        got.append(lax.ppermute(pick(quarters, (zl + d) % 4), ("zh", "zl", "x"), pairs))
    up1, down1, g0, g1, g2, g3 = tie(up1, down1, *got)

    up2, down2 = shift(up1, RING, 8, 1), shift(down1, RING, 8, -1)
    turned = jnp.zeros((4, part, rows), bf16)
    for d, piece in enumerate((g0, g1, g2, g3)):
        turned = lax.dynamic_update_index_in_dim(turned, piece, (zl - d) % 4, 0)
    turned = turned.reshape(4 * part, rows)
    across = [turned] + [shift(turned, "x", 4, k) for k in (1, 2, 3)]
    up3, down3 = shift(up2, RING, 8, 1), shift(down2, RING, 8, -1)
    up3, down3, *across = tie(up3, down3, *across)
    last = split_ways(jnp.where(core == 0, up3, down3), 1)

    right_late, _, _ = tie(right_basis, up3, down3)
    right_own = lax.all_gather(right_late, RING).reshape(2, 4, *right_basis.shape)

    gradient = jnp.zeros((8, rows, cols), bf16)
    blocks = ((0, grad), (1, up1), (-1, down1), (2, up2), (-2, down2), (3, up3), (-3, down3))
    for s, block in blocks + ((4, last),):
        gradient = lax.dynamic_update_index_in_dim(gradient, block, (z - s) % 8, 0)
    gradient = gradient.reshape(2, 4, rows, cols)

    away = shift(turn_left(place, across, gradient, True), "core", 2, 1)
    mine = turn_left(place, across, gradient, False)
    total = mine[0] + away[0]
    for d in (1, 2, 3):
        total = total + shift((mine[d] + away[d]).astype(bf16), "y", 4, d).astype(f32)
    rotated_in = total.astype(bf16)
    wide = [rotated_in] + [shift(rotated_in, "x", 4, d) for d in (1, 2, 3)]
    right_own, *_ = tie(right_own, *wide)
    right_far = shift(right_own, "core", 2, 1)
    moments, _ = tie(jnp.stack([first_moment, second_moment]), rotated_in)

    moments = moments.reshape(2, 4, part, cols)
    near = [lax.dynamic_index_in_dim(moments, zl, 1, keepdims=False)]
    for e in (1, 2, 3):
        near.append(
            shift(lax.dynamic_index_in_dim(moments, (zl + e) % 4, 1, keepdims=False), "zl", 4, e)
        )
    near = jnp.concatenate(near, axis=2)

    rotated, *sent = turn_right(place, wide, right_own, right_far)
    for d in (1, 2, 3):
        rotated = rotated + shift(sent[d - 1], "y", 4, d).astype(f32)
    normed = adam_moments(rotated, near[0], near[1])[2]

    normed, late = tie(normed, rotated.astype(bf16))
    normed = [normed] + [shift(normed, "y", 4, d) for d in (1, 2, 3)]
    pieces = [late[:, e * cols : (e + 1) * cols] for e in range(4)]
    pieces = [pieces[0]] + [shift(pieces[e], "zl", 4, -e) for e in (1, 2, 3)]
    *normed, p0, p1, p2, p3 = tie(*normed, *pieces)

    early, later = turn_back(place, normed, right_own, right_far)
    *later, p0, p1, p2, p3 = tie(*later, p0, p1, p2, p3)
    home = jnp.zeros((4, part, cols), bf16)
    for e, piece in enumerate((p0, p1, p2, p3)):
        home = lax.dynamic_update_index_in_dim(home, piece, (zl + e) % 4, 0)
    first_new, second_new, _ = adam_moments(
        home.reshape(rows, cols).astype(f32), first_moment, second_moment
    )
    update = []
    for total, *sent in (early, later):
        for d in (1, 2, 3):
            total = total + shift(sent[d - 1], "x", 4, d).astype(f32)
        back = total.astype(bf16)
        full = [back] + [shift(back, "y", 4, d) for d in (1, 2, 3)]
        near, plus, minus, most = turn_left_back(
            place, across, full, shift(jnp.stack(full), "core", 2, 1)
        )
        plus, minus = shift(plus, RING, 8, 1).astype(f32), shift(minus, RING, 8, -1).astype(f32)
        most = split_ways(most, 2).astype(f32)
        ahead, behind = jnp.where(core == 0, most, 0.0), jnp.where(core == 0, 0.0, most)
        ahead = shift((near[1] + plus[0] + ahead).astype(bf16), RING, 8, 2)
        behind = shift((near[2] + minus[0] + behind).astype(bf16), RING, 8, -2)
        update.append(near[0] + plus[1] + minus[1] + ahead.astype(f32) + behind.astype(f32))
    update = jnp.concatenate(update, axis=1)

    return (update, first_new, second_new)


def solution(mesh):
    names = ("y", "zh", "core", "zl", "x")
    fine = Mesh(mesh.devices.reshape(4, 2, 2, 4, 4), names)
    spec = P(("y", "zh", "core"), ("zl", "x"))
    return jax.shard_map(
        body, mesh=fine, in_specs=(spec,) * 5, out_specs=(spec,) * 3, check_vma=False
    )
```

```python
import jax
import jax.numpy as jnp
from jax import lax
from jax.experimental import pallas as pl
from jax.experimental.pallas import tpu as pltpu
from jax.sharding import Mesh
from jax.sharding import PartitionSpec as P

beta_one = 0.9
beta_two = 0.95
corr_one = 1.0 - 0.9**10
corr_two = 1.0 - 0.95**10
eps_value = 1e-08

RING = ("zh", "zl")


def shift(arr, axes, size, by):
    return lax.ppermute(arr, axes, [(i, (i + by) % size) for i in range(size)])


def to_three(send, axis):
    got = {d: shift(send(d), axis, 4, d) for d in (2, 1, 3)}
    return [got[1], got[2], got[3]]


def split_ways(arr, by):
    pairs = []
    for core in range(2):
        for z in range(8):
            to = (z + (by, -by)[core]) % 8
            pairs.append(((z // 4 * 2 + core) * 4 + z % 4, (to // 4 * 2 + core) * 4 + to % 4))
    return lax.ppermute(arr, ("zh", "core", "zl"), pairs)


def pick(arr, index):
    return lax.dynamic_index_in_dim(arr, index, 0, keepdims=False)


def tie(*values):
    return lax.optimization_barrier(values)


def turn_right(place, wide, right_own, right_far):
    rows, cols = wide[0].shape
    part = rows // 4

    def kernel(at, w0, w1, w2, w3, own, far, mine, far1, far2, far3, held, total):
        x, y, core = at[0], at[1], at[3]

        @pl.when(pl.program_id(0) == 0)
        def _():
            for d, ref in enumerate((w0, w1, w2, w3)):
                held[lax.rem(x + 4 - d, 4)] = ref[...]

        acc = jnp.zeros((rows, cols), jnp.float32)
        for which, ref in ((core, own), (1 - core, far)):
            for h in range(2):
                acc += jnp.dot(held[2 * h + which], ref[h, 0], preferred_element_type=jnp.float32)
        total[...] = acc.reshape(4, part, cols)
        mine[...] = total[y]
        for d, ref in ((1, far1), (2, far2), (3, far3)):
            ref[...] = total[lax.rem(y + d, 4)].astype(jnp.bfloat16)

    whole = pl.BlockSpec((rows, cols), lambda e, at: (0, 0))
    block = pl.BlockSpec((2, 1, cols, cols), lambda e, at: (0, lax.rem(at[2] + 4 - e, 4), 0, 0))
    out = pl.BlockSpec((part, cols), lambda e, at: (0, e))
    return pl.pallas_call(
        kernel,
        grid_spec=pltpu.PrefetchScalarGridSpec(
            num_scalar_prefetch=1,
            grid=(4,),
            in_specs=[whole] * 4 + [block] * 2,
            out_specs=[out] * 4,
            scratch_shapes=[
                pltpu.VMEM((4, rows, cols), jnp.bfloat16),
                pltpu.VMEM((4, part, cols), jnp.float32),
            ],
        ),
        out_shape=[jax.ShapeDtypeStruct((part, 4 * cols), jnp.float32)]
        + [jax.ShapeDtypeStruct((part, 4 * cols), jnp.bfloat16)] * 3,
        compiler_params=pltpu.CompilerParams(vmem_limit_bytes=40 * 2**20),
        cost_estimate=pl.CostEstimate(
            flops=32 * rows * cols * cols, bytes_accessed=32 * cols * cols, transcendentals=0
        ),
    )(place, *wide, right_own, right_far)


def turn_left(place, across, gradient, other):
    rows, cols = gradient.shape[2:]

    def kernel(at, l0, l1, l2, l3, right, out, left):
        @pl.when(pl.program_id(0) == 0)
        def _():
            for d, ref in enumerate((l0, l1, l2, l3)):
                left[lax.rem(at[0] + 4 - d, 4)] = ref[...]

        which = 1 - at[3] if other else at[3]
        acc = jnp.zeros((rows, cols), jnp.float32)
        for h in range(2):
            acc += jnp.dot(left[2 * h + which], right[h, 0], preferred_element_type=jnp.float32)
        out[0] = acc

    return pl.pallas_call(
        kernel,
        grid_spec=pltpu.PrefetchScalarGridSpec(
            num_scalar_prefetch=1,
            grid=(4,),
            in_specs=[
                *[pl.BlockSpec((rows, rows), lambda j, at: (0, 0))] * 4,
                pl.BlockSpec((2, 1, rows, cols), lambda j, at: (0, lax.rem(at[1] + j, 4), 0, 0)),
            ],
            out_specs=pl.BlockSpec((1, rows, cols), lambda j, at: (j, 0, 0)),
            scratch_shapes=[pltpu.VMEM((4, rows, rows), jnp.bfloat16)],
        ),
        out_shape=jax.ShapeDtypeStruct((4, rows, cols), jnp.float32),
        compiler_params=pltpu.CompilerParams(vmem_limit_bytes=40 * 2**20),
        cost_estimate=pl.CostEstimate(
            flops=16 * rows * rows * cols, bytes_accessed=16 * rows * cols, transcendentals=0
        ),
    )(place, *across, gradient)


def turn_back(place, normed, right_own, right_far):
    part, long = normed[0].shape
    rows, cols = 4 * part, long // 4
    width = cols // 2

    def kernel(at, n0, n1, n2, n3, own, far, *rest):
        outs, held = rest[:8], rest[8]
        x, y, zl, core = at[0], at[1], at[2], at[3]
        h = pl.program_id(0)

        @pl.when(h == 0)
        def _():
            for d, ref in enumerate((n0, n1, n2, n3)):
                held[lax.rem(y + 4 - d, 4)] = ref[...]

        for which, ref in ((core, own), (1 - core, far)):
            acc = jnp.zeros((rows, cols), jnp.float32)
            for e in range(4):
                acc += lax.dot_general(
                    held[:, :, e * cols : (e + 1) * cols].reshape(rows, cols),
                    ref[0, lax.rem(zl + 4 - e, 4)],
                    (((1,), (1,)), ((), ())),
                    preferred_element_type=jnp.float32,
                )
            slot = lax.rem(2 * h + which + 4 - x, 4)
            for d in range(4):

                @pl.when(slot == d)
                def _():
                    for half in range(2):
                        to = outs[half * 4 + d]
                        to[...] = acc[:, half * width : (half + 1) * width].astype(to.dtype)

    whole = pl.BlockSpec((part, long), lambda h, at: (0, 0))
    block = pl.BlockSpec((1, 4, cols, cols), lambda h, at: (h, 0, 0, 0))
    out = pl.BlockSpec((rows, width), lambda h, at: (0, 0))
    kinds = (jnp.float32, jnp.bfloat16, jnp.bfloat16, jnp.bfloat16) * 2
    outs = pl.pallas_call(
        kernel,
        grid_spec=pltpu.PrefetchScalarGridSpec(
            num_scalar_prefetch=1,
            grid=(2,),
            in_specs=[whole] * 4 + [block] * 2,
            out_specs=[out] * 8,
            scratch_shapes=[pltpu.VMEM((4, part, long), jnp.bfloat16)],
        ),
        out_shape=[jax.ShapeDtypeStruct((rows, width), kind) for kind in kinds],
        compiler_params=pltpu.CompilerParams(vmem_limit_bytes=40 * 2**20),
        cost_estimate=pl.CostEstimate(
            flops=32 * rows * cols * cols, bytes_accessed=32 * cols * cols, transcendentals=0
        ),
    )(place, *normed, right_own, right_far)
    return outs[:4], outs[4:]


def turn_left_back(place, across, own, far):
    rows = across[0].shape[0]
    width = own[0].shape[1]

    def kernel(at, l0, l1, l2, l3, o0, o1, o2, o3, other, near, plus, minus, most, held, left):
        x, y, zl, core, z = at[0], at[1], at[2], at[3], at[4]
        for d in range(4):
            slot = lax.rem(y + 4 - d, 4)
            held[core, slot] = (o0, o1, o2, o3)[d][...]
            held[1 - core, slot] = other[d]
            left[lax.rem(x + 4 - d, 4)] = (l0, l1, l2, l3)[d][...].T
        for t, (ref, k) in {
            3: (plus, 0), 5: (minus, 0), 4: (most, None), 1: (plus, 1), 7: (minus, 1),
            2: (near, 1), 6: (near, 2), 0: (near, 0),
        }.items():
            to = lax.rem(z + t, 8)
            acc = jnp.zeros((rows, width), jnp.float32)
            for c in range(2):
                acc += jnp.dot(
                    left[2 * lax.div(to, 4) + c], held[c, lax.rem(to, 4)], preferred_element_type=jnp.float32
                )
            if k is None:
                ref[...] = acc.astype(ref.dtype)
            else:
                ref[k] = acc.astype(ref.dtype)

    vmem = pl.BlockSpec(memory_space=pltpu.VMEM)
    return pl.pallas_call(
        kernel,
        in_specs=[pl.BlockSpec(memory_space=pltpu.SMEM)] + [vmem] * 9,
        out_specs=[vmem] * 4,
        scratch_shapes=[
            pltpu.VMEM((2, 4, rows, width), jnp.bfloat16),
            pltpu.VMEM((4, rows, rows), jnp.bfloat16),
        ],
        out_shape=[
            jax.ShapeDtypeStruct((3, rows, width), jnp.float32),
            jax.ShapeDtypeStruct((2, rows, width), jnp.bfloat16),
            jax.ShapeDtypeStruct((2, rows, width), jnp.bfloat16),
            jax.ShapeDtypeStruct((rows, width), jnp.bfloat16),
        ],
        compiler_params=pltpu.CompilerParams(vmem_limit_bytes=40 * 2**20),
        cost_estimate=pl.CostEstimate(
            flops=32 * rows * rows * width, bytes_accessed=32 * rows * width, transcendentals=0
        ),
    )(place, *across, *own, far)


def adam_moments(rotated, first_moment, second_moment):
    first_new = beta_one * first_moment + (1.0 - beta_one) * rotated
    second_new = beta_two * second_moment + (1.0 - beta_two) * rotated * rotated
    normed = (first_new / corr_one / (jnp.sqrt(second_new / corr_two) + eps_value)).astype(
        jnp.bfloat16
    )
    return (first_new, second_new, normed)


def body(grad, left_basis, right_basis, first_moment, second_moment):
    f32, bf16 = jnp.float32, jnp.bfloat16
    y, zh, core = lax.axis_index("y"), lax.axis_index("zh"), lax.axis_index("core")
    zl, x = lax.axis_index("zl"), lax.axis_index("x")
    z = zh * 4 + zl
    rows, cols = grad.shape
    lead, part = left_basis.shape[1], left_basis.shape[1] // 4

    place = jnp.stack([x, y, zl, core, z]).astype(jnp.int32)

    up1, down1 = shift(grad, RING, 8, 1), shift(grad, RING, 8, -1)
    quarters = left_basis.T.reshape(4, part, rows)
    got = []
    for d in range(4):
        pairs = []
        for zs in range(2):
            for ls in range(4):
                for xs in range(4):
                    to = ((xs // 2) * 4 + (ls + d) % 4) * 4 + zs * 2 + xs % 2
                    pairs.append(((zs * 4 + ls) * 4 + xs, to))
        got.append(lax.ppermute(pick(quarters, (zl + d) % 4), ("zh", "zl", "x"), pairs))
    up1, down1, g0, g1, g2, g3 = tie(up1, down1, *got)

    up2, down2 = shift(up1, RING, 8, 1), shift(down1, RING, 8, -1)
    turned = jnp.zeros((4, part, rows), bf16)
    for d, piece in enumerate((g0, g1, g2, g3)):
        turned = lax.dynamic_update_index_in_dim(turned, piece, (zl - d) % 4, 0)
    turned = turned.reshape(4 * part, rows)
    across = [turned] + [shift(turned, "x", 4, k) for k in (1, 2, 3)]
    up3, down3 = shift(up2, RING, 8, 1), shift(down2, RING, 8, -1)
    up3, down3, *across = tie(up3, down3, *across)
    last = split_ways(jnp.where(core == 0, up3, down3), 1)

    right_late, _, _ = tie(right_basis, up3, down3)
    right_own = lax.all_gather(right_late, RING).reshape(2, 4, *right_basis.shape)

    gradient = jnp.zeros((8, rows, cols), bf16)
    blocks = ((0, grad), (1, up1), (-1, down1), (2, up2), (-2, down2), (3, up3), (-3, down3))
    for s, block in blocks + ((4, last),):
        gradient = lax.dynamic_update_index_in_dim(gradient, block, (z - s) % 8, 0)
    gradient = gradient.reshape(2, 4, rows, cols)

    away = shift(turn_left(place, across, gradient, True), "core", 2, 1)
    mine = turn_left(place, across, gradient, False)
    total = mine[0] + away[0]
    for piece in to_three(lambda d: (mine[d] + away[d]).astype(bf16), "y"):
        total = total + piece.astype(f32)
    rotated_in = total.astype(bf16)
    wide = [rotated_in] + to_three(lambda d: rotated_in, "x")
    right_own, *_ = tie(right_own, *wide)
    right_far = shift(right_own, "core", 2, 1)
    moments, _ = tie(jnp.stack([first_moment, second_moment]), rotated_in)

    moments = moments.reshape(2, 4, part, cols)
    near = [lax.dynamic_index_in_dim(moments, zl, 1, keepdims=False)]
    for e in (1, 2, 3):
        near.append(
            shift(lax.dynamic_index_in_dim(moments, (zl + e) % 4, 1, keepdims=False), "zl", 4, e)
        )
    near = jnp.concatenate(near, axis=2)

    rotated, *sent = turn_right(place, wide, right_own, right_far)
    for piece in to_three(lambda d: sent[d - 1], "y"):
        rotated = rotated + piece.astype(f32)
    normed = adam_moments(rotated, near[0], near[1])[2]

    normed, late = tie(normed, rotated.astype(bf16))
    normed = [normed] + to_three(lambda d, block=normed: block, "y")
    pieces = [late[:, e * cols : (e + 1) * cols] for e in range(4)]
    pieces = [pieces[0]] + [shift(pieces[e], "zl", 4, -e) for e in (1, 2, 3)]
    *normed, p0, p1, p2, p3 = tie(*normed, *pieces)

    early, later = turn_back(place, normed, right_own, right_far)
    *later, p0, p1, p2, p3 = tie(*later, p0, p1, p2, p3)
    home = jnp.zeros((4, part, cols), bf16)
    for e, piece in enumerate((p0, p1, p2, p3)):
        home = lax.dynamic_update_index_in_dim(home, piece, (zl + e) % 4, 0)
    first_new, second_new, _ = adam_moments(
        home.reshape(rows, cols).astype(f32), first_moment, second_moment
    )
    update = []
    for total, *sent in (early, later):
        for piece in to_three(lambda d: sent[d - 1], "x"):
            total = total + piece.astype(f32)
        back = total.astype(bf16)
        full = [back] + to_three(lambda d: back, "y")
        near, plus, minus, most = turn_left_back(
            place, across, full, shift(jnp.stack(full), "core", 2, 1)
        )
        plus, minus = shift(plus, RING, 8, 1).astype(f32), shift(minus, RING, 8, -1).astype(f32)
        most = split_ways(most, 2).astype(f32)
        ahead, behind = jnp.where(core == 0, most, 0.0), jnp.where(core == 0, 0.0, most)
        ahead = shift((near[1] + plus[0] + ahead).astype(bf16), RING, 8, 2)
        behind = shift((near[2] + minus[0] + behind).astype(bf16), RING, 8, -2)
        update.append(near[0] + plus[1] + minus[1] + ahead.astype(f32) + behind.astype(f32))
    update = jnp.concatenate(update, axis=1)

    return (update, first_new, second_new)


def solution(mesh):
    names = ("y", "zh", "core", "zl", "x")
    fine = Mesh(mesh.devices.reshape(4, 2, 2, 4, 4), names)
    spec = P(("y", "zh", "core"), ("zl", "x"))
    return jax.shard_map(
        body, mesh=fine, in_specs=(spec,) * 5, out_specs=(spec,) * 3, check_vma=False
    )
```
